32 devices in a mesh: row: 8 (over z, core), col: 4 (over y, x).
Axes of the slice: x: 2, y: 2, z: 4, core: 2. Of those that a mesh axis runs over, the one named last changes fastest.
Arguments:
- voxels: bfloat16 [8, 8, 16384], P('row', 'col'), may hold values from -6 to 6
- norm_gain: float32 [64], replicated, may hold values from 0.25 to 1.75
- in_weight: bfloat16 [64, 256], replicated, may hold values from -0.75 to 0.75
- conv_weight: float32 [6, 4, 128], replicated, may hold values from -3 to 3
- conv_bias: float32 [6, 128], replicated, may hold values from -3 to 3
- x_weight: bfloat16 [6, 128, 36], replicated, may hold values from -0.5 to 0.5
- dt_weight: float32 [6, 4, 128], replicated, may hold values from -3 to 3
- dt_bias: float32 [6, 128], replicated, may hold values from -6 to -1
- a_rate: float32 [6, 128, 16], replicated, may hold values from 0.1 to 4
- skip_gain: float32 [6, 128], replicated, may hold values from 0.5 to 1.5
- out_weight: bfloat16 [128, 64], replicated, may hold values from -0.5 to 0.5
Outputs:
- mixed: bfloat16 [8, 8, 16384], P('row', 'col')
The draws below stay inside these ranges and needn't reach their ends.
All inputs are finite; a program needn't handle non-finite values.
Results may differ from the reference program's by a relative error of at most 0.013.
Values may be sent and summed in bfloat16 or wider, within the bound.
A program may use at most 64 MiB of HBM per device.

```python
import math
import jax
import jax.numpy as jnp
from jax import lax

C = 64
E = 128
N = 16
R = 4
K = 4
Z = 256
X = 8
Y = 8


def shard_levels(own_key, dims, shards, low, high):
    loudness, own = 1.0, jax.random.fold_in(own_key, 6)
    for axis_at, shards_of in shards:
        steps = jnp.exp(jax.random.uniform(jax.random.fold_in(own, axis_at), (shards_of,), jnp.float32, low / len(shards), high / len(shards)))
        loudness = loudness * jnp.repeat(steps, dims[axis_at] // shards_of).reshape([-1 if axis == axis_at else 1 for axis in range(len(dims))])
    return loudness


def scatter_about(rng, shape, deviation, bound, shards=(), kind=jnp.bfloat16):
    drawn = jax.random.normal(rng, shape, jnp.float32) * deviation
    if len(shards) > 0:
        drawn = shard_levels(rng, shape, shards, -0.22, 0.18) * drawn
    return jnp.clip(drawn, min=-bound, max=bound).astype(kind)


def setup_inputs(seed: int = 0) -> dict:
    key_list = jax.random.split(jax.random.key(seed), 12)
    voxels = scatter_about(key_list[0], (X, Y, Z * C), 1.0, 6.0, ((0, 8), (1, 4)))
    norm_gain = jnp.clip(1.0 + 0.15 * jax.random.normal(key_list[1], (C,), jnp.float32), 0.25, 1.75)
    in_weight = scatter_about(key_list[2], (C, 2 * E), C ** -0.5, 0.75)
    conv_weight = scatter_about(key_list[3], (6, K, E), K ** -0.5, 3.0, (), jnp.float32)
    conv_bias = scatter_about(key_list[4], (6, E), 0.5, 3.0, (), jnp.float32)
    x_weight = scatter_about(key_list[5], (6, E, R + 2 * N), E ** -0.5, 0.5)
    dt_weight = scatter_about(key_list[6], (6, R, E), R ** -0.5, 3.0, (), jnp.float32)
    dt_bias = jnp.clip(jax.random.uniform(key_list[7], (6, E), jnp.float32, -6.0, -1.0), -6.0, -1.0)
    a_rate = jnp.clip(jnp.exp(jax.random.uniform(key_list[8], (6, E, N), jnp.float32, math.log(0.1), math.log(4.0))), 0.1, 4.0)
    skip_gain = jnp.clip(jax.random.uniform(key_list[9], (6, E), jnp.float32, 0.5, 1.5), 0.5, 1.5)
    out_weight = scatter_about(key_list[10], (E, C), E ** -0.5, 0.5)
    return {"voxels": voxels, "norm_gain": norm_gain, "in_weight": in_weight, "conv_weight": conv_weight, "conv_bias": conv_bias, "x_weight": x_weight, "dt_weight": dt_weight, "dt_bias": dt_bias, "a_rate": a_rate, "skip_gain": skip_gain, "out_weight": out_weight}


def activation(line_rows, index, conv_weight, conv_bias):
    kernel = conv_weight.shape[1]
    length = line_rows.shape[1]
    values = line_rows.astype(jnp.float32)
    padded = jnp.pad(values, ((0, 0), (kernel - 1, 0), (0, 0)))
    preact = conv_bias[index].astype(jnp.float32)
    for offset in range(kernel):
        preact = preact + conv_weight[index, offset] * padded[:, offset:offset + length]
    return jax.nn.silu(preact).astype(jnp.bfloat16)

def run_direction(line_rows, index, reverse, conv_weight, conv_bias, x_weight, dt_weight, dt_bias, a_rate, skip_gain):
    ordered = line_rows[:, ::-1] if reverse else line_rows
    activated = activation(ordered, index, conv_weight, conv_bias)
    state_n = a_rate.shape[2]
    rank = dt_weight.shape[1]
    projected = jnp.einsum('mle,ef->mlf', activated.astype(jnp.float32), x_weight[index].astype(jnp.float32))
    low_rank = projected[..., :rank]
    b_select = projected[..., rank:rank + state_n]
    c_select = projected[..., rank + state_n:]
    step_size = jax.nn.softplus(jnp.einsum('mlr,re->mle', low_rank, dt_weight[index], precision=lax.Precision.HIGHEST) + dt_bias[index])
    decay_rate = a_rate[index]
    act_float = activated.astype(jnp.float32)

    def advance(carried, inputs):
        step_now, act_now, b_now, c_now = inputs
        decays = jnp.exp(-step_now[:, :, None] * decay_rate)
        carried = decays * carried + (step_now * act_now)[:, :, None] * b_now[:, None, :]
        return (carried, lax.optimization_barrier(jnp.sum(carried * c_now[:, None, :], axis=2)))
    inputs = (jnp.swapaxes(step_size, 0, 1), jnp.swapaxes(act_float, 0, 1), jnp.swapaxes(b_select, 0, 1), jnp.swapaxes(c_select, 0, 1))
    start = jnp.zeros((line_rows.shape[0], line_rows.shape[2], state_n), jnp.float32)
    _, results = lax.scan(advance, start, inputs)
    results = jnp.swapaxes(results, 0, 1) + skip_gain[index] * act_float
    return results[:, ::-1] if reverse else results

def both_ways(line_rows, index, *params):
    return run_direction(line_rows, index, False, *params) + run_direction(line_rows, index + 1, True, *params)

def reference(voxels, norm_gain, in_weight, conv_weight, conv_bias, x_weight, dt_weight, dt_bias, a_rate, skip_gain, out_weight):
    params = (conv_weight, conv_bias, x_weight, dt_weight, dt_bias, a_rate, skip_gain)
    values = voxels.reshape(X, Y, Z, C).astype(jnp.float32)
    normed = (values * lax.rsqrt(lax.optimization_barrier(jnp.mean(values * values, axis=-1, keepdims=True)) + 1e-05) * norm_gain).astype(jnp.bfloat16)
    flat_rows = normed.reshape(-1, C)
    inner = jnp.dot(flat_rows, in_weight[:, :E], preferred_element_type=jnp.float32).astype(jnp.bfloat16).reshape(X, Y, Z, E)
    gate = jnp.dot(flat_rows, in_weight[:, E:], preferred_element_type=jnp.float32)
    silu_gate = jax.nn.silu(gate)
    along_z = both_ways(inner.reshape(X * Y, Z, E), 0, *params).reshape(X, Y, Z, E)
    along_y = both_ways(inner.transpose(0, 2, 1, 3).reshape(X * Z, Y, E), 2, *params)
    sum_y = along_y.reshape(X, Z, Y, E).transpose(0, 2, 1, 3).astype(jnp.bfloat16)
    along_x = both_ways(inner.transpose(1, 2, 0, 3).reshape(Y * Z, X, E), 4, *params)
    along_x = along_x.reshape(Y, Z, X, E).transpose(2, 0, 1, 3)
    sum_xy = (sum_y.astype(jnp.float32) + along_x).astype(jnp.bfloat16)
    far_hidden = (sum_xy.reshape(-1, E).astype(jnp.float32) * silu_gate).astype(jnp.bfloat16)
    far_part = jnp.dot(far_hidden, out_weight, preferred_element_type=jnp.float32).astype(jnp.bfloat16)
    near_hidden = (along_z.reshape(-1, E) * silu_gate).astype(jnp.bfloat16)
    mixed = (jnp.dot(near_hidden, out_weight, preferred_element_type=jnp.float32) + far_part.astype(jnp.float32)).astype(jnp.bfloat16)
    return mixed.reshape(X, Y, Z * C)
```

```python
import functools

import jax
import jax.numpy as jnp
from jax import lax
from jax.experimental import pallas as pl
from jax.experimental.pallas import tpu as pltpu
from jax.sharding import PartitionSpec as P

MESH = pl.DeviceIdType.MESH
LOG2E = 1.4426950408889634
F32 = jnp.float32
BF16 = jnp.bfloat16


def silu(x):
    half = 0.5 * x
    return half + half * jnp.tanh(half)


def softplus(x):
    u = jnp.exp(-jnp.abs(x))
    return jnp.maximum(x, 0.0) + jnp.where(u < 1e-3, u - 0.5 * u * u, jnp.log(1.0 + u))


def column(tile, lane):
    return jnp.broadcast_to(tile[:, lane : lane + 1], tile.shape)


def kernel(
    sizes,
    vox_ref,
    gain_ref,
    inw_ref,
    convw_ref,
    convb_ref,
    xw_ref,
    dtw_ref,
    dtb_ref,
    rate_ref,
    skip_ref,
    outw_ref,
    out_ref,
    w4,
    ow2,
    xwp,
    dtwp,
    ratep,
    rates,
    nb,
    xs,
    yin,
    xin,
    yret,
    xret,
    yfar,
    xfar,
    inn,
    sgate,
    lstep,
    lu,
    lproj,
    lout,
    zinner,
    comb,
    zstep,
    zu,
    zproj,
    zskip,
    zout,
    zgate,
    acc,
    ysend,
    yrecv,
    xsend,
    xrecv,
    yrsend,
    yrrecv,
    xrsend,
    xrrecv,
):
    nrow, ncol, y_loc, half_z, zpy, zpx, width, inner, state, rank = sizes
    my_row, my_col = lax.axis_index("row"), lax.axis_index("col")
    z_cells = 2 * half_z

    barrier = pltpu.get_barrier_semaphore()
    for k in range(1, ncol):
        peer = lax.rem(my_col + k, ncol)
        pl.semaphore_signal(barrier, inc=1, device_id=(my_row, peer), device_id_type=MESH)
    for k in range(1, nrow):
        peer = lax.rem(my_row + k, nrow)
        pl.semaphore_signal(barrier, inc=1, device_id=(peer, my_col), device_id_type=MESH)

    values = vox_ref[...].astype(F32)
    squares = values * values
    lane = lax.broadcasted_iota(jnp.int32, values.shape, 1)
    low_half = lane < width
    mean_a = jnp.sum(jnp.where(low_half, squares, 0.0), axis=1, keepdims=True) * (1.0 / width)
    mean_b = jnp.sum(jnp.where(low_half, 0.0, squares), axis=1, keepdims=True) * (1.0 / width)
    scale = jnp.where(low_half, lax.rsqrt(mean_a + 1e-5), lax.rsqrt(mean_b + 1e-5))
    normed = values * scale * gain_ref[...]
    nb[...] = normed.astype(BF16).reshape(nb.shape)
    for r in range(nrow):
        pieces = [
            normed[y * half_z + r * zpx : y * half_z + (r + 1) * zpx] for y in range(y_loc)
        ]
        xs[r] = jnp.concatenate(pieces, axis=0).astype(BF16)

    pl.semaphore_wait(barrier, ncol - 1 + nrow - 1)

    def y_go(k):
        peer = lax.rem(my_col + k, ncol)
        return pltpu.make_async_remote_copy(
            src_ref=nb.at[:, pl.ds(pl.multiple_of(peer * zpy, zpy), zpy), :],
            dst_ref=yin.at[pl.ds(my_col * y_loc, y_loc)],
            send_sem=ysend.at[k],
            recv_sem=yrecv.at[k],
            device_id=(my_row, peer),
            device_id_type=MESH,
        )

    def x_go(k):
        peer = lax.rem(my_row + k, nrow)
        return pltpu.make_async_remote_copy(
            src_ref=xs.at[peer],
            dst_ref=xin.at[my_row],
            send_sem=xsend.at[k],
            recv_sem=xrecv.at[k],
            device_id=(peer, my_col),
            device_id_type=MESH,
        )

    def y_back(k):
        peer = lax.rem(my_col + k, ncol)
        return pltpu.make_async_remote_copy(
            src_ref=yret.at[pl.ds(peer * y_loc, y_loc)],
            dst_ref=yfar.at[my_col],
            send_sem=yrsend.at[k],
            recv_sem=yrrecv.at[k],
            device_id=(my_row, peer),
            device_id_type=MESH,
        )

    def x_back(k):
        peer = lax.rem(my_row + k, nrow)
        return pltpu.make_async_remote_copy(
            src_ref=xret.at[peer],
            dst_ref=xfar.at[my_row],
            send_sem=xrsend.at[k],
            recv_sem=xrrecv.at[k],
            device_id=(peer, my_col),
            device_id_type=MESH,
        )

    for k in range(1, ncol):
        y_go(k).start()
    for k in range(1, nrow):
        x_go(k).start()

    w4[...] = jnp.zeros_like(w4)
    w4[0:width, 0:inner] = inw_ref[:, 0:inner]
    w4[width : 2 * width, inner : 2 * inner] = inw_ref[:, 0:inner]
    w4[0:width, 2 * inner : 3 * inner] = inw_ref[:, inner : 2 * inner]
    w4[width : 2 * width, 3 * inner : 4 * inner] = inw_ref[:, inner : 2 * inner]
    ow2[...] = jnp.zeros_like(ow2)
    ow2[0:inner, 0:width] = outw_ref[...]
    ow2[inner : 2 * inner, width : 2 * width] = outw_ref[...]
    xwp[...] = jnp.zeros_like(xwp)
    xwp[:, :, 0 : rank + 2 * state] = xw_ref[...]
    dtwp[...] = jnp.zeros_like(dtwp)
    dtwp[:, 0:rank, :] = dtw_ref[...]
    for d in range(6):
        ratep[...] = jnp.zeros_like(ratep)
        ratep[:, 0:state] = rate_ref[d] * (-LOG2E)
        rates[d] = ratep[...].T[0:state]

    rows = 2 * 2 * y_loc
    front = rows // 2
    row8 = lax.broadcasted_iota(jnp.int32, (rows, inner), 0)
    forward8 = row8 < front
    lowhalf8 = lax.rem(row8, 2) == 0

    full = jnp.dot(nb[...].reshape(y_loc * half_z, 2 * width), w4[...], preferred_element_type=F32)
    zgate[...] = silu(full[:, 2 * inner :])
    for par in range(2):
        own = full[:, par * inner : (par + 1) * inner].astype(BF16).astype(F32)
        for y in range(y_loc):
            piece = own[y * half_z : (y + 1) * half_z]
            for direction in range(2):
                for low in range(2):
                    start = par * rows + direction * front + y * 2 + low
                    zinner[pl.ds(start, half_z, stride=2 * rows), :] = piece
    taps = convw_ref.shape[1]
    pad = taps - 1
    comb[0 : pad * rows, :] = jnp.zeros((pad * rows, inner), F32)

    @pl.loop(0, z_cells // 8)
    def _(block):
        for i in range(8):
            t = block * 8 + i
            up = zinner[pl.ds(pl.multiple_of(t * rows, rows), rows), :]
            down = zinner[pl.ds(pl.multiple_of((z_cells - 1 - t) * rows, rows), rows), :]
            comb[pl.ds(pl.multiple_of((t + pad) * rows, rows), rows), :] = jnp.where(
                forward8, up, down
            )

    def by_dir(a, b):
        return jnp.where(forward8, a, b)

    zconv = [by_dir(convw_ref[0, k : k + 1, :], convw_ref[1, k : k + 1, :]) for k in range(taps)]
    zbias = by_dir(convb_ref[0:1, :], convb_ref[1:2, :])
    zdtb = by_dir(dtb_ref[0:1, :], dtb_ref[1:2, :])
    zskipw = jnp.where(lowhalf8, by_dir(skip_ref[0:1, :], skip_ref[1:2, :]), 0.0)
    chunk = 32

    @pl.loop(0, z_cells // chunk)
    def _(block):
        base = pl.multiple_of(block * (chunk * rows), chunk * rows)
        pre = zbias[None]
        for k in range(taps):
            tap = comb[pl.ds(base + k * rows, chunk * rows), :]
            pre = pre + zconv[k][None] * tap.reshape(chunk, rows, inner)
        act_b = silu(pre).reshape(chunk * rows, inner).astype(BF16)
        act = act_b.astype(F32)
        row = lax.broadcasted_iota(jnp.int32, (chunk * rows, inner), 0)
        forward = lax.rem(row, rows) < front
        low = lax.rem(row, 2) == 0
        p0 = jnp.dot(act_b, xwp[0], preferred_element_type=F32)
        p1 = jnp.dot(act_b, xwp[1], preferred_element_type=F32)
        proj = jnp.where(forward, p0, p1)
        s0 = jnp.dot(proj, dtwp[0], precision=lax.Precision.HIGHEST, preferred_element_type=F32)
        s1 = jnp.dot(proj, dtwp[1], precision=lax.Precision.HIGHEST, preferred_element_type=F32)
        step = jnp.where(forward, s0, s1).reshape(chunk, rows, inner) + zdtb[None]
        step = softplus(step).reshape(chunk * rows, inner)
        here = pl.ds(base, chunk * rows)
        zstep[here, :] = step
        zu[here, :] = step * act
        zproj[here, :] = jnp.where(low, proj, pltpu.roll(proj, inner - state // 2, axis=1))
        zskip[here, :] = (act.reshape(chunk, rows, inner) * zskipw[None]).reshape(
            chunk * rows, inner
        )

    def lines(src_ref, ret_ref, d):
        length, pairs = src_ref.shape[0], src_ref.shape[1]
        count = 2 * pairs
        total = length * count
        both = jnp.dot(
            src_ref[...].reshape(length * pairs, 2 * width), w4[...], preferred_element_type=F32
        )
        inn[0:pad] = jnp.zeros((pad, count, inner), F32)
        inn[pad + length :] = jnp.zeros((pad, count, inner), F32)
        for par in range(2):
            part = both[:, par * inner : (par + 1) * inner].astype(BF16).astype(F32)
            inn[pad : pad + length, par * pairs : (par + 1) * pairs, :] = part.reshape(
                length, pairs, inner
            )
            gate = both[:, (2 + par) * inner : (3 + par) * inner]
            sgate[:, par * pairs : (par + 1) * pairs, :] = silu(gate).reshape(length, pairs, inner)
        for direction in range(2):
            e = d + direction
            pre = convb_ref[e : e + 1, :][None]
            for k in range(taps):
                first = k if direction == 0 else 2 * pad - k
                pre = pre + convw_ref[e, k : k + 1, :][None] * inn[first : first + length]
            act_b = silu(pre).reshape(total, inner).astype(BF16)
            act = act_b.astype(F32)
            proj = jnp.dot(act_b, xwp[e], preferred_element_type=F32)
            low = jnp.dot(
                proj, dtwp[e], precision=lax.Precision.HIGHEST, preferred_element_type=F32
            )
            step = softplus(low + dtb_ref[e : e + 1, :])
            lstep[...] = step.reshape(lstep.shape)
            lu[...] = (step * act).reshape(lu.shape)
            lproj[...] = proj.reshape(lproj.shape)
            skipped = (act * skip_ref[e : e + 1, :]).reshape(lout.shape)
            if direction == 0:
                lout[...] = skipped
            else:
                lout[...] += skipped

            @pl.loop(0, count // 8)
            def _(group):
                at = pl.ds(pl.multiple_of(group * 8, 8), 8)
                held = [jnp.zeros((8, inner), F32) for _ in range(state)]
                for i in range(length):
                    t = i if direction == 0 else length - 1 - i
                    step_t, u_t, proj_t = lstep[t, at, :], lu[t, at, :], lproj[t, at, :]
                    result = lout[t, at, :]
                    for n in range(state):
                        inflow = u_t * column(proj_t, rank + n)
                        if i == 0:
                            held[n] = inflow
                        else:
                            decay = jnp.exp2(step_t * rates[e, n : n + 1, :])
                            held[n] = decay * held[n] + inflow
                        result = result + held[n] * column(proj_t, rank + state + n)
                    lout[t, at, :] = result

        hidden = [
            (lout[:, par * pairs : (par + 1) * pairs, :] * sgate[:, par * pairs : (par + 1) * pairs, :])
            .reshape(length * pairs, inner)
            .astype(BF16)
            for par in range(2)
        ]
        far = jnp.dot(jnp.concatenate(hidden, axis=1), ow2[...], preferred_element_type=F32)
        ret_ref[...] = far.astype(BF16).reshape(ret_ref.shape)

    for y in range(y_loc):
        yin[my_col * y_loc + y] = nb[y, pl.ds(pl.multiple_of(my_col * zpy, zpy), zpy), :]
    for k in range(1, ncol):
        y_go(k).wait()
    lines(yin, yret, 2)
    for k in range(1, ncol):
        y_back(k).start()
    xin[my_row] = xs[my_row]
    for k in range(1, nrow):
        x_go(k).wait()
    lines(xin, xret, 4)
    for k in range(1, nrow):
        x_back(k).start()

    halves = state // 2
    zrate = [
        jnp.where(
            lowhalf8,
            by_dir(rates[0, n : n + 1, :], rates[1, n : n + 1, :]),
            by_dir(rates[0, halves + n : halves + n + 1, :], rates[1, halves + n : halves + n + 1, :]),
        )
        for n in range(halves)
    ]
    unroll = 8

    def advance(block, held):
        held = list(held)
        for i in range(unroll):
            t = block * unroll + i
            at = pl.ds(pl.multiple_of(t * rows, rows), rows)
            step_t, u_t, proj_t = zstep[at, :], zu[at, :], zproj[at, :]
            result = zskip[at, :]
            for n in range(halves):
                decay = jnp.exp2(step_t * zrate[n])
                held[n] = decay * held[n] + u_t * column(proj_t, rank + n)
                result = result + held[n] * column(proj_t, rank + state + n)
            zout[pl.ds(pl.multiple_of(t * rows, rows), front), :] = result[0:front]
            zout[pl.ds((z_cells - 1 - t) * rows + front, front), :] = result[front:]
        return tuple(held)

    lax.fori_loop(
        0,
        z_cells // unroll,
        advance,
        tuple(jnp.zeros((rows, inner), F32) for _ in range(halves)),
    )

    near = []
    for par in range(2):
        pieces = []
        for y in range(y_loc):
            total = None
            for direction in range(2):
                for low in range(2):
                    start = par * rows + direction * front + y * 2 + low
                    part = zout[pl.ds(start, half_z, stride=2 * rows), :]
                    total = part if total is None else total + part
            pieces.append(total)
        along = jnp.concatenate(pieces, axis=0)
        near.append((along * zgate[:, par * inner : (par + 1) * inner]).astype(BF16))
    acc[...] = jnp.dot(jnp.concatenate(near, axis=1), ow2[...], preferred_element_type=F32)

    yfar[my_col] = yret[pl.ds(my_col * y_loc, y_loc)]
    xfar[my_row] = xret[my_row]
    for k in range(1, ncol):
        y_back(k).wait()
    for c in range(ncol):
        for y in range(y_loc):
            acc[y * half_z + c * zpy : y * half_z + (c + 1) * zpy, :] += yfar[c, y].astype(F32)
    for k in range(1, nrow):
        x_back(k).wait()
    for r in range(nrow):
        part = xfar[r].astype(F32)
        for y in range(y_loc):
            acc[y * half_z + r * zpx : y * half_z + (r + 1) * zpx, :] += part[
                y * zpx : (y + 1) * zpx
            ]
    out_ref[...] = acc[...].astype(BF16)


def solution(mesh):
    nrow, ncol = mesh.shape["row"], mesh.shape["col"]

    def local(
        voxels,
        norm_gain,
        in_weight,
        conv_weight,
        conv_bias,
        x_weight,
        dt_weight,
        dt_bias,
        a_rate,
        skip_gain,
        out_weight,
    ):
        width = norm_gain.shape[0]
        inner = out_weight.shape[0]
        state, rank = a_rate.shape[2], dt_weight.shape[1]
        x_loc, y_loc, merged = voxels.shape
        assert x_loc == 1 and y_loc == 2
        z_cells = merged // width
        half_z = z_cells // 2
        zpy, zpx = half_z // ncol, half_z // nrow
        y_full = ncol * y_loc
        assert y_full == nrow and zpy == y_loc * zpx
        tokens = y_loc * half_z
        sizes = (nrow, ncol, y_loc, half_z, zpy, zpx, width, inner, state, rank)
        pairs = voxels.reshape(tokens, 2 * width)
        gain = jnp.concatenate([norm_gain, norm_gain]).reshape(1, 2 * width)
        line = (nrow, 2 * zpy, inner)
        zrows = 4 * y_loc * z_cells
        taps = conv_weight.shape[1]
        vmem = pl.BlockSpec(memory_space=pltpu.VMEM)
        out = pl.pallas_call(
            functools.partial(kernel, sizes),
            out_shape=jax.ShapeDtypeStruct((tokens, 2 * width), BF16),
            in_specs=[vmem] * 11,
            out_specs=vmem,
            scratch_shapes=[
                pltpu.VMEM((2 * width, 4 * inner), BF16),
                pltpu.VMEM((2 * inner, 2 * width), BF16),
                pltpu.VMEM((6, inner, 128), BF16),
                pltpu.VMEM((6, 128, inner), F32),
                pltpu.VMEM((inner, 128), F32),
                pltpu.VMEM((6, state, inner), F32),
                pltpu.VMEM((y_loc, half_z, 2 * width), BF16),
                pltpu.VMEM((nrow, y_loc * zpx, 2 * width), BF16),
                pltpu.VMEM((y_full, zpy, 2 * width), BF16),
                pltpu.VMEM((nrow, y_loc * zpx, 2 * width), BF16),
                pltpu.VMEM((y_full, zpy, 2 * width), BF16),
                pltpu.VMEM((nrow, y_loc * zpx, 2 * width), BF16),
                pltpu.VMEM((ncol, y_loc, zpy, 2 * width), BF16),
                pltpu.VMEM((nrow, y_loc * zpx, 2 * width), BF16),
                pltpu.VMEM((nrow + 2 * (taps - 1), 2 * zpy, inner), F32),
                pltpu.VMEM(line, F32),
                pltpu.VMEM(line, F32),
                pltpu.VMEM(line, F32),
                pltpu.VMEM(line, F32),
                pltpu.VMEM(line, F32),
                pltpu.VMEM((zrows, inner), F32),
                pltpu.VMEM((zrows + (taps - 1) * 4 * y_loc, inner), F32),
                pltpu.VMEM((zrows, inner), F32),
                pltpu.VMEM((zrows, inner), F32),
                pltpu.VMEM((zrows, inner), F32),
                pltpu.VMEM((zrows, inner), F32),
                pltpu.VMEM((zrows, inner), F32),
                pltpu.VMEM((tokens, 2 * inner), F32),
                pltpu.VMEM((tokens, 2 * width), F32),
                pltpu.SemaphoreType.DMA((ncol,)),
                pltpu.SemaphoreType.DMA((ncol,)),
                pltpu.SemaphoreType.DMA((nrow,)),
                pltpu.SemaphoreType.DMA((nrow,)),
                pltpu.SemaphoreType.DMA((ncol,)),
                pltpu.SemaphoreType.DMA((ncol,)),
                pltpu.SemaphoreType.DMA((nrow,)),
                pltpu.SemaphoreType.DMA((nrow,)),
            ],
            compiler_params=pltpu.CompilerParams(
                collective_id=0, has_side_effects=True, vmem_limit_bytes=40 * 1024 * 1024
            ),
        )(
            pairs,
            gain,
            in_weight,
            conv_weight,
            conv_bias,
            x_weight,
            dt_weight,
            dt_bias,
            a_rate,
            skip_gain,
            out_weight,
        )
        return out.reshape(voxels.shape)

    in_specs = (P("row", "col", None), P(), P(), P(), P(), P(), P(), P(), P(), P(), P())
    return jax.shard_map(
        local, mesh=mesh, in_specs=in_specs, out_specs=P("row", "col", None), check_vma=False
    )
```

```python
import functools

import jax
import jax.numpy as jnp
from jax import lax
from jax.experimental import pallas as pl
from jax.experimental.pallas import tpu as pltpu
from jax.sharding import PartitionSpec as P

MESH = pl.DeviceIdType.MESH
LOG2E = 1.4426950408889634
F32 = jnp.float32
BF16 = jnp.bfloat16


def silu(x):
    half = 0.5 * x
    return half + half * jnp.tanh(half)


def softplus(x):
    u = jnp.exp(-jnp.abs(x))
    return jnp.maximum(x, 0.0) + jnp.where(u < 1e-3, u - 0.5 * u * u, jnp.log(1.0 + u))


def dot_t(a, b):
    return lax.dot_general(a, b, (((1,), (1,)), ((), ())), preferred_element_type=F32)


def split_lanes(proj):
    half = proj.shape[1] // 2
    high = proj.astype(BF16).astype(F32)
    lane = lax.broadcasted_iota(jnp.int32, proj.shape, 1)
    return jnp.where(lane < half, high, pltpu.roll(proj - high, half, axis=1)).astype(BF16)


def kernel(
    sizes,
    vox_ref,
    gain_ref,
    inw_ref,
    convw_ref,
    convb_ref,
    xw_ref,
    dtw_ref,
    dtb_ref,
    rate_ref,
    skip_ref,
    outw_ref,
    out_ref,
    w4,
    ow2,
    xwp,
    dtwp,
    rates,
    spread,
    zspread,
    lspread,
    nb,
    xs,
    yin,
    xin,
    yret,
    xret,
    yfar,
    xfar,
    inn,
    sgate,
    lstep,
    lu,
    lout,
    zinner,
    comb,
    zstep,
    zu,
    zskip,
    zout,
    zgate,
    acc,
    ysend,
    yrecv,
    xsend,
    xrecv,
    yrsend,
    yrrecv,
    xrsend,
    xrrecv,
):
    nrow, ncol, y_loc, half_z, zpy, zpx, width, inner, state, rank = sizes
    my_row, my_col = lax.axis_index("row"), lax.axis_index("col")
    z_cells = 2 * half_z

    barrier = pltpu.get_barrier_semaphore()
    for k in range(1, ncol):
        peer = lax.rem(my_col + k, ncol)
        pl.semaphore_signal(barrier, inc=1, device_id=(my_row, peer), device_id_type=MESH)
    for k in range(1, nrow):
        peer = lax.rem(my_row + k, nrow)
        pl.semaphore_signal(barrier, inc=1, device_id=(peer, my_col), device_id_type=MESH)

    values = vox_ref[...].astype(F32)
    squares = values * values
    lane = lax.broadcasted_iota(jnp.int32, values.shape, 1)
    low_half = lane < width
    mean_a = jnp.sum(jnp.where(low_half, squares, 0.0), axis=1, keepdims=True) * (1.0 / width)
    mean_b = jnp.sum(jnp.where(low_half, 0.0, squares), axis=1, keepdims=True) * (1.0 / width)
    scale = jnp.where(low_half, lax.rsqrt(mean_a + 1e-5), lax.rsqrt(mean_b + 1e-5))
    normed = values * scale * jnp.concatenate([gain_ref[...], gain_ref[...]], axis=1)
    nb[...] = normed.astype(BF16).reshape(nb.shape)
    for r in range(nrow):
        pieces = [
            normed[y * half_z + r * zpx : y * half_z + (r + 1) * zpx] for y in range(y_loc)
        ]
        xs[r] = jnp.concatenate(pieces, axis=0).astype(BF16)

    pl.semaphore_wait(barrier, ncol - 1 + nrow - 1)

    def y_go(k):
        peer = lax.rem(my_col + k, ncol)
        return pltpu.make_async_remote_copy(
            src_ref=nb.at[:, pl.ds(pl.multiple_of(peer * zpy, zpy), zpy), :],
            dst_ref=yin.at[pl.ds(my_col * y_loc, y_loc)],
            send_sem=ysend.at[k],
            recv_sem=yrecv.at[k],
            device_id=(my_row, peer),
            device_id_type=MESH,
        )

    def x_go(k):
        peer = lax.rem(my_row + k, nrow)
        return pltpu.make_async_remote_copy(
            src_ref=xs.at[peer],
            dst_ref=xin.at[my_row],
            send_sem=xsend.at[k],
            recv_sem=xrecv.at[k],
            device_id=(peer, my_col),
            device_id_type=MESH,
        )

    def y_back(k):
        peer = lax.rem(my_col + k, ncol)
        return pltpu.make_async_remote_copy(
            src_ref=yret.at[pl.ds(peer * y_loc, y_loc)],
            dst_ref=yfar.at[my_col],
            send_sem=yrsend.at[k],
            recv_sem=yrrecv.at[k],
            device_id=(my_row, peer),
            device_id_type=MESH,
        )

    def x_back(k):
        peer = lax.rem(my_row + k, nrow)
        return pltpu.make_async_remote_copy(
            src_ref=xret.at[peer],
            dst_ref=xfar.at[my_row],
            send_sem=xrsend.at[k],
            recv_sem=xrrecv.at[k],
            device_id=(peer, my_col),
            device_id_type=MESH,
        )

    for k in range(1, ncol):
        y_go(k).start()
    for k in range(1, nrow):
        x_go(k).start()

    w4[...] = jnp.zeros_like(w4)
    w4[0:width, 0:inner] = inw_ref[:, 0:inner]
    w4[width : 2 * width, inner : 2 * inner] = inw_ref[:, 0:inner]
    w4[0:width, 2 * inner : 3 * inner] = inw_ref[:, inner : 2 * inner]
    w4[width : 2 * width, 3 * inner : 4 * inner] = inw_ref[:, inner : 2 * inner]
    ow2[...] = jnp.zeros_like(ow2)
    ow2[0:width, 0:inner] = outw_ref[...]
    ow2[width : 2 * width, inner : 2 * inner] = outw_ref[...]
    xwp[...] = jnp.zeros_like(xwp)
    xwp[:, 0 : rank + 2 * state, :] = xw_ref[...]
    dtwp[...] = jnp.zeros_like(dtwp)
    dtwp[:, 0:rank, :] = dtw_ref[...]
    rates[...] = rate_ref[...] * (-LOG2E)
    source = lax.broadcasted_iota(jnp.int32, (inner, inner), 0)
    for n in range(2 * state):
        hit = (source == rank + n) | (source == inner // 2 + rank + n)
        spread[:, n * inner : (n + 1) * inner] = jnp.where(hit, 1.0, 0.0).astype(BF16)

    rows = 2 * 2 * y_loc
    front = rows // 2
    row8 = lax.broadcasted_iota(jnp.int32, (rows, inner), 0)
    forward8 = row8 < front
    lowhalf8 = lax.rem(row8, 2) == 0

    full = jnp.dot(nb[...].reshape(y_loc * half_z, 2 * width), w4[...], preferred_element_type=F32)
    zgate[...] = silu(full[:, 2 * inner :])
    for par in range(2):
        own = full[:, par * inner : (par + 1) * inner].astype(BF16).astype(F32)
        for y in range(y_loc):
            piece = own[y * half_z : (y + 1) * half_z]
            for direction in range(2):
                for low in range(2):
                    start = par * rows + direction * front + y * 2 + low
                    zinner[pl.ds(start, half_z, stride=2 * rows), :] = piece
    taps = convw_ref.shape[1]
    pad = taps - 1
    comb[0 : pad * rows, :] = jnp.zeros((pad * rows, inner), F32)

    @pl.loop(0, z_cells // 8)
    def _(block):
        for i in range(8):
            t = block * 8 + i
            up = zinner[pl.ds(pl.multiple_of(t * rows, rows), rows), :]
            down = zinner[pl.ds(pl.multiple_of((z_cells - 1 - t) * rows, rows), rows), :]
            comb[pl.ds(pl.multiple_of((t + pad) * rows, rows), rows), :] = jnp.where(
                forward8, up, down
            )

    def by_dir(a, b):
        return jnp.where(forward8, a, b)

    zconv = [by_dir(convw_ref[0, k : k + 1, :], convw_ref[1, k : k + 1, :]) for k in range(taps)]
    zbias = by_dir(convb_ref[0:1, :], convb_ref[1:2, :])
    zdtb = by_dir(dtb_ref[0:1, :], dtb_ref[1:2, :])
    zskipw = jnp.where(lowhalf8, by_dir(skip_ref[0:1, :], skip_ref[1:2, :]), 0.0)
    chunk = 32

    @pl.loop(0, z_cells // chunk)
    def _(block):
        base = pl.multiple_of(block * (chunk * rows), chunk * rows)
        pre = zbias[None]
        for k in range(taps):
            tap = comb[pl.ds(base + k * rows, chunk * rows), :]
            pre = pre + zconv[k][None] * tap.reshape(chunk, rows, inner)
        act_b = silu(pre).reshape(chunk * rows, inner).astype(BF16)
        act = act_b.astype(F32)
        row = lax.broadcasted_iota(jnp.int32, (chunk * rows, inner), 0)
        forward = lax.rem(row, rows) < front
        low = lax.rem(row, 2) == 0
        p0 = dot_t(act_b, xwp[0])
        p1 = dot_t(act_b, xwp[1])
        proj = jnp.where(forward, p0, p1)
        s0 = jnp.dot(proj, dtwp[0], precision=lax.Precision.HIGHEST, preferred_element_type=F32)
        s1 = jnp.dot(proj, dtwp[1], precision=lax.Precision.HIGHEST, preferred_element_type=F32)
        step = jnp.where(forward, s0, s1).reshape(chunk, rows, inner) + zdtb[None]
        step = softplus(step).reshape(chunk * rows, inner)
        here = pl.ds(base, chunk * rows)
        zstep[here, :] = step
        zu[here, :] = step * act
        parts = split_lanes(jnp.where(low, proj, pltpu.roll(proj, inner - state // 2, axis=1)))
        wide = state // 2 * inner
        for g in range(2):
            zspread[here, g * wide : (g + 1) * wide] = jnp.dot(
                parts, spread[:, 2 * g * wide : (2 * g + 1) * wide], preferred_element_type=F32
            )
        zskip[here, :] = (act.reshape(chunk, rows, inner) * zskipw[None]).reshape(
            chunk * rows, inner
        )

    def lines(src_ref, ret_ref, d):
        length, pairs = src_ref.shape[0], src_ref.shape[1]
        count = 2 * pairs
        total = length * count
        both = jnp.dot(
            src_ref[...].reshape(length * pairs, 2 * width), w4[...], preferred_element_type=F32
        )
        inn[0:pad] = jnp.zeros((pad, count, inner), F32)
        inn[pad + length :] = jnp.zeros((pad, count, inner), F32)
        for par in range(2):
            part = both[:, par * inner : (par + 1) * inner].astype(BF16).astype(F32)
            inn[pad : pad + length, par * pairs : (par + 1) * pairs, :] = part.reshape(
                length, pairs, inner
            )
            gate = both[:, (2 + par) * inner : (3 + par) * inner]
            sgate[:, par * pairs : (par + 1) * pairs, :] = silu(gate).reshape(length, pairs, inner)
        for direction in range(2):
            e = d + direction
            pre = convb_ref[e : e + 1, :][None]
            for k in range(taps):
                first = k if direction == 0 else 2 * pad - k
                pre = pre + convw_ref[e, k : k + 1, :][None] * inn[first : first + length]
            act_b = silu(pre).reshape(total, inner).astype(BF16)
            act = act_b.astype(F32)
            proj = dot_t(act_b, xwp[e])
            low = jnp.dot(
                proj, dtwp[e], precision=lax.Precision.HIGHEST, preferred_element_type=F32
            )
            step = softplus(low + dtb_ref[e : e + 1, :])
            lstep[...] = step.reshape(lstep.shape)
            lu[...] = (step * act).reshape(lu.shape)
            parts = split_lanes(proj)
            for n in range(0, 2 * state, 4):
                block = slice(n * inner, (n + 4) * inner)
                lspread[:, :, block] = jnp.dot(
                    parts, spread[:, block], preferred_element_type=F32
                ).reshape(length, count, 4 * inner)
            skipped = (act * skip_ref[e : e + 1, :]).reshape(lout.shape)
            if direction == 0:
                lout[...] = skipped
            else:
                lout[...] += skipped

            @pl.loop(0, count // 8)
            def _(group):
                at = pl.ds(pl.multiple_of(group * 8, 8), 8)
                held = [jnp.zeros((8, inner), F32) for _ in range(state)]
                for i in range(length):
                    t = i if direction == 0 else length - 1 - i
                    step_t, u_t = lstep[t, at, :], lu[t, at, :]
                    result = lout[t, at, :]
                    for n in range(state):
                        inflow = u_t * lspread[t, at, n * inner : (n + 1) * inner]
                        if i == 0:
                            held[n] = inflow
                        else:
                            decay = jnp.exp2(step_t * rates[e, n : n + 1, :])
                            held[n] = decay * held[n] + inflow
                        m = state + n
                        result = result + held[n] * lspread[t, at, m * inner : (m + 1) * inner]
                    lout[t, at, :] = result

        hidden = [
            (lout[:, par * pairs : (par + 1) * pairs, :] * sgate[:, par * pairs : (par + 1) * pairs, :])
            .reshape(length * pairs, inner)
            .astype(BF16)
            for par in range(2)
        ]
        far = dot_t(jnp.concatenate(hidden, axis=1), ow2[...])
        ret_ref[...] = far.astype(BF16).reshape(ret_ref.shape)

    for y in range(y_loc):
        yin[my_col * y_loc + y] = nb[y, pl.ds(pl.multiple_of(my_col * zpy, zpy), zpy), :]
    for k in range(1, ncol):
        y_go(k).wait()
    lines(yin, yret, 2)
    for k in range(1, ncol):
        y_back(k).start()
    xin[my_row] = xs[my_row]
    for k in range(1, nrow):
        x_go(k).wait()
    lines(xin, xret, 4)
    for k in range(1, nrow):
        x_back(k).start()

    halves = state // 2
    zrate = [
        jnp.where(
            lowhalf8,
            by_dir(rates[0, n : n + 1, :], rates[1, n : n + 1, :]),
            by_dir(rates[0, halves + n : halves + n + 1, :], rates[1, halves + n : halves + n + 1, :]),
        )
        for n in range(halves)
    ]
    unroll = 8

    def advance(block, held):
        held = list(held)
        for i in range(unroll):
            t = block * unroll + i
            at = pl.ds(pl.multiple_of(t * rows, rows), rows)
            step_t, u_t = zstep[at, :], zu[at, :]
            result = zskip[at, :]
            for n in range(halves):
                decay = jnp.exp2(step_t * zrate[n])
                held[n] = decay * held[n] + u_t * zspread[at, n * inner : (n + 1) * inner]
                m = halves + n
                result = result + held[n] * zspread[at, m * inner : (m + 1) * inner]
            zout[pl.ds(pl.multiple_of(t * rows, rows), front), :] = result[0:front]
            zout[pl.ds((z_cells - 1 - t) * rows + front, front), :] = result[front:]
        return tuple(held)

    lax.fori_loop(
        0,
        z_cells // unroll,
        advance,
        tuple(jnp.zeros((rows, inner), F32) for _ in range(halves)),
    )

    near = []
    for par in range(2):
        pieces = []
        for y in range(y_loc):
            total = None
            for direction in range(2):
                for low in range(2):
                    start = par * rows + direction * front + y * 2 + low
                    part = zout[pl.ds(start, half_z, stride=2 * rows), :]
                    total = part if total is None else total + part
            pieces.append(total)
        along = jnp.concatenate(pieces, axis=0)
        near.append((along * zgate[:, par * inner : (par + 1) * inner]).astype(BF16))
    acc[...] = dot_t(jnp.concatenate(near, axis=1), ow2[...])

    yfar[my_col] = yret[pl.ds(my_col * y_loc, y_loc)]
    xfar[my_row] = xret[my_row]
    for k in range(1, ncol):
        y_back(k).wait()
    for c in range(ncol):
        for y in range(y_loc):
            acc[y * half_z + c * zpy : y * half_z + (c + 1) * zpy, :] += yfar[c, y].astype(F32)
    for k in range(1, nrow):
        x_back(k).wait()
    for r in range(nrow):
        part = xfar[r].astype(F32)
        for y in range(y_loc):
            acc[y * half_z + r * zpx : y * half_z + (r + 1) * zpx, :] += part[
                y * zpx : (y + 1) * zpx
            ]
    out_ref[...] = acc[...].astype(BF16)


def solution(mesh):
    nrow, ncol = mesh.shape["row"], mesh.shape["col"]

    def local(
        voxels,
        norm_gain,
        in_weight,
        conv_weight,
        conv_bias,
        x_weight,
        dt_weight,
        dt_bias,
        a_rate,
        skip_gain,
        out_weight,
    ):
        width = norm_gain.shape[0]
        inner = out_weight.shape[0]
        state, rank = a_rate.shape[2], dt_weight.shape[1]
        x_loc, y_loc, merged = voxels.shape
        assert x_loc == 1 and y_loc == 2
        z_cells = merged // width
        half_z = z_cells // 2
        zpy, zpx = half_z // ncol, half_z // nrow
        y_full = ncol * y_loc
        assert y_full == nrow and zpy == y_loc * zpx
        tokens = y_loc * half_z
        sizes = (nrow, ncol, y_loc, half_z, zpy, zpx, width, inner, state, rank)
        pairs = voxels.reshape(tokens, 2 * width)
        gain = norm_gain.reshape(1, width)
        line = (nrow, 2 * zpy, inner)
        zrows = 4 * y_loc * z_cells
        taps = conv_weight.shape[1]
        vmem = pl.BlockSpec(memory_space=pltpu.VMEM)
        out = pl.pallas_call(
            functools.partial(kernel, sizes),
            out_shape=jax.ShapeDtypeStruct((tokens, 2 * width), BF16),
            in_specs=[vmem] * 11,
            out_specs=vmem,
            scratch_shapes=[
                pltpu.VMEM((2 * width, 4 * inner), BF16),
                pltpu.VMEM((2 * width, 2 * inner), BF16),
                pltpu.VMEM((6, 128, inner), BF16),
                pltpu.VMEM((6, 128, inner), F32),
                pltpu.VMEM((6, state, inner), F32),
                pltpu.VMEM((inner, 2 * state * inner), BF16),
                pltpu.VMEM((zrows, state * inner), F32),
                pltpu.VMEM((nrow, 2 * zpy, 2 * state * inner), F32),
                pltpu.VMEM((y_loc, half_z, 2 * width), BF16),
                pltpu.VMEM((nrow, y_loc * zpx, 2 * width), BF16),
                pltpu.VMEM((y_full, zpy, 2 * width), BF16),
                pltpu.VMEM((nrow, y_loc * zpx, 2 * width), BF16),
                pltpu.VMEM((y_full, zpy, 2 * width), BF16),
                pltpu.VMEM((nrow, y_loc * zpx, 2 * width), BF16),
                pltpu.VMEM((ncol, y_loc, zpy, 2 * width), BF16),
                pltpu.VMEM((nrow, y_loc * zpx, 2 * width), BF16),
                pltpu.VMEM((nrow + 2 * (taps - 1), 2 * zpy, inner), F32),
                pltpu.VMEM(line, F32),
                pltpu.VMEM(line, F32),
                pltpu.VMEM(line, F32),
                pltpu.VMEM(line, F32),
                pltpu.VMEM((zrows, inner), F32),
                pltpu.VMEM((zrows + (taps - 1) * 4 * y_loc, inner), F32),
                pltpu.VMEM((zrows, inner), F32),
                pltpu.VMEM((zrows, inner), F32),
                pltpu.VMEM((zrows, inner), F32),
                pltpu.VMEM((zrows, inner), F32),
                pltpu.VMEM((tokens, 2 * inner), F32),
                pltpu.VMEM((tokens, 2 * width), F32),
                pltpu.SemaphoreType.DMA((ncol,)),
                pltpu.SemaphoreType.DMA((ncol,)),
                pltpu.SemaphoreType.DMA((nrow,)),
                pltpu.SemaphoreType.DMA((nrow,)),
                pltpu.SemaphoreType.DMA((ncol,)),
                pltpu.SemaphoreType.DMA((ncol,)),
                pltpu.SemaphoreType.DMA((nrow,)),
                pltpu.SemaphoreType.DMA((nrow,)),
            ],
            compiler_params=pltpu.CompilerParams(
                collective_id=0, has_side_effects=True, vmem_limit_bytes=52 * 1024 * 1024
            ),
        )(
            pairs,
            gain,
            in_weight,
            conv_weight,
            conv_bias,
            jnp.swapaxes(x_weight, 1, 2),
            dt_weight,
            dt_bias,
            jnp.swapaxes(a_rate, 1, 2),
            skip_gain,
            out_weight.T,
        )
        return out.reshape(voxels.shape)

    in_specs = (P("row", "col", None), P(), P(), P(), P(), P(), P(), P(), P(), P(), P())
    return jax.shard_map(
        local, mesh=mesh, in_specs=in_specs, out_specs=P("row", "col", None), check_vma=False
    )
```

```python
import functools

import jax
import jax.numpy as jnp
from jax import lax
from jax.experimental import pallas as pl
from jax.experimental.pallas import tpu as pltpu
from jax.sharding import PartitionSpec as P

MESH = pl.DeviceIdType.MESH
LOG2E = 1.4426950408889634
F32 = jnp.float32
BF16 = jnp.bfloat16


def silu(x):
    half = 0.5 * x
    return half + half * jnp.tanh(half)


def softplus(x):
    u = jnp.exp(-jnp.abs(x))
    return jnp.maximum(x, 0.0) + jnp.where(u < 1e-3, u - 0.5 * u * u, jnp.log(1.0 + u))


def dot_t(a, b):
    return lax.dot_general(a, b, (((1,), (1,)), ((), ())), preferred_element_type=F32)


def split_lanes(proj):
    half = proj.shape[1] // 2
    high = proj.astype(BF16).astype(F32)
    lane = lax.broadcasted_iota(jnp.int32, proj.shape, 1)
    return jnp.where(lane < half, high, pltpu.roll(proj - high, half, axis=1)).astype(BF16)


def kernel(
    sizes,
    vox_ref,
    gain_ref,
    inw_hbm,
    convw_hbm,
    convb_hbm,
    xw_hbm,
    dtw_hbm,
    dtb_hbm,
    rate_hbm,
    skip_hbm,
    outw_hbm,
    out_ref,
    inw_ref,
    convw_ref,
    convb_ref,
    xw_ref,
    dtw_ref,
    dtb_ref,
    rate_ref,
    skip_ref,
    outw_ref,
    wsem,
    w4,
    ow2,
    xwp,
    dtwp,
    rates,
    spread,
    zspread,
    lspread,
    nb,
    xs,
    yin,
    xin,
    yret,
    xret,
    yfar,
    xfar,
    inn,
    sgate,
    lstep,
    lu,
    lout,
    zinner,
    comb,
    zstep,
    zu,
    zskip,
    zout,
    zgate,
    acc,
    ysend,
    yrecv,
    xsend,
    xrecv,
    yrsend,
    yrrecv,
    xrsend,
    xrrecv,
):
    nrow, ncol, y_loc, half_z, zpy, zpx, width, inner, state, rank = sizes
    my_row, my_col = lax.axis_index("row"), lax.axis_index("col")
    z_cells = 2 * half_z

    weights = (
        (inw_hbm, inw_ref),
        (convw_hbm, convw_ref),
        (convb_hbm, convb_ref),
        (xw_hbm, xw_ref),
        (dtw_hbm, dtw_ref),
        (dtb_hbm, dtb_ref),
        (rate_hbm, rate_ref),
        (skip_hbm, skip_ref),
        (outw_hbm, outw_ref),
    )
    fetches = [
        pltpu.make_async_copy(far, near, wsem.at[i]) for i, (far, near) in enumerate(weights)
    ]
    for fetch in fetches:
        fetch.start()
    barrier = pltpu.get_barrier_semaphore()
    for k in range(1, ncol):
        peer = lax.rem(my_col + k, ncol)
        pl.semaphore_signal(barrier, inc=1, device_id=(my_row, peer), device_id_type=MESH)
    for k in range(1, nrow):
        peer = lax.rem(my_row + k, nrow)
        pl.semaphore_signal(barrier, inc=1, device_id=(peer, my_col), device_id_type=MESH)

    values = vox_ref[...].astype(F32)
    squares = values * values
    lane = lax.broadcasted_iota(jnp.int32, values.shape, 1)
    low_half = lane < width
    mean_a = jnp.sum(jnp.where(low_half, squares, 0.0), axis=1, keepdims=True) * (1.0 / width)
    mean_b = jnp.sum(jnp.where(low_half, 0.0, squares), axis=1, keepdims=True) * (1.0 / width)
    scale = jnp.where(low_half, lax.rsqrt(mean_a + 1e-5), lax.rsqrt(mean_b + 1e-5))
    normed = values * scale * jnp.concatenate([gain_ref[...], gain_ref[...]], axis=1)
    nb[...] = normed.astype(BF16).reshape(nb.shape)
    for r in range(nrow):
        pieces = [
            normed[y * half_z + r * zpx : y * half_z + (r + 1) * zpx] for y in range(y_loc)
        ]
        xs[r] = jnp.concatenate(pieces, axis=0).astype(BF16)

    pl.semaphore_wait(barrier, ncol - 1 + nrow - 1)

    def y_go(k):
        peer = lax.rem(my_col + k, ncol)
        return pltpu.make_async_remote_copy(
            src_ref=nb.at[:, pl.ds(pl.multiple_of(peer * zpy, zpy), zpy), :],
            dst_ref=yin.at[pl.ds(my_col * y_loc, y_loc)],
            send_sem=ysend.at[k],
            recv_sem=yrecv.at[k],
            device_id=(my_row, peer),
            device_id_type=MESH,
        )

    def x_go(k):
        peer = lax.rem(my_row + k, nrow)
        return pltpu.make_async_remote_copy(
            src_ref=xs.at[peer],
            dst_ref=xin.at[my_row],
            send_sem=xsend.at[k],
            recv_sem=xrecv.at[k],
            device_id=(peer, my_col),
            device_id_type=MESH,
        )

    def y_back(k):
        peer = lax.rem(my_col + k, ncol)
        return pltpu.make_async_remote_copy(
            src_ref=yret.at[pl.ds(peer * y_loc, y_loc)],
            dst_ref=yfar.at[my_col],
            send_sem=yrsend.at[k],
            recv_sem=yrrecv.at[k],
            device_id=(my_row, peer),
            device_id_type=MESH,
        )

    def x_back(k):
        peer = lax.rem(my_row + k, nrow)
        return pltpu.make_async_remote_copy(
            src_ref=xret.at[peer],
            dst_ref=xfar.at[my_row],
            send_sem=xrsend.at[k],
            recv_sem=xrrecv.at[k],
            device_id=(peer, my_col),
            device_id_type=MESH,
        )

    for k in range(1, ncol):
        y_go(k).start()
    for k in range(1, nrow):
        x_go(k).start()

    for fetch in fetches:
        fetch.wait()
    w4[...] = jnp.zeros_like(w4)
    w4[0:width, 0:inner] = inw_ref[:, 0:inner]
    w4[width : 2 * width, inner : 2 * inner] = inw_ref[:, 0:inner]
    w4[0:width, 2 * inner : 3 * inner] = inw_ref[:, inner : 2 * inner]
    w4[width : 2 * width, 3 * inner : 4 * inner] = inw_ref[:, inner : 2 * inner]
    ow2[...] = jnp.zeros_like(ow2)
    ow2[0:width, 0:inner] = outw_ref[...]
    ow2[width : 2 * width, inner : 2 * inner] = outw_ref[...]
    xwp[...] = jnp.zeros_like(xwp)
    xwp[:, 0 : rank + 2 * state, :] = xw_ref[...]
    dtwp[...] = jnp.zeros_like(dtwp)
    dtwp[:, 0:rank, :] = dtw_ref[...]
    rates[...] = rate_ref[...] * (-LOG2E)
    source = lax.broadcasted_iota(jnp.int32, (inner, inner), 0)
    for n in range(2 * state):
        hit = (source == rank + n) | (source == inner // 2 + rank + n)
        spread[:, n * inner : (n + 1) * inner] = jnp.where(hit, 1.0, 0.0).astype(BF16)

    rows = 2 * 2 * y_loc
    front = rows // 2
    row8 = lax.broadcasted_iota(jnp.int32, (rows, inner), 0)
    forward8 = row8 < front
    lowhalf8 = lax.rem(row8, 2) == 0

    full = jnp.dot(nb[...].reshape(y_loc * half_z, 2 * width), w4[...], preferred_element_type=F32)
    zgate[...] = silu(full[:, 2 * inner :])
    for par in range(2):
        own = full[:, par * inner : (par + 1) * inner].astype(BF16).astype(F32)
        for y in range(y_loc):
            piece = own[y * half_z : (y + 1) * half_z]
            for direction in range(2):
                for low in range(2):
                    start = par * rows + direction * front + y * 2 + low
                    zinner[pl.ds(start, half_z, stride=2 * rows), :] = piece
    taps = convw_ref.shape[1]
    pad = taps - 1
    comb[0 : pad * rows, :] = jnp.zeros((pad * rows, inner), F32)

    @pl.loop(0, z_cells // 8)
    def _(block):
        for i in range(8):
            t = block * 8 + i
            up = zinner[pl.ds(pl.multiple_of(t * rows, rows), rows), :]
            down = zinner[pl.ds(pl.multiple_of((z_cells - 1 - t) * rows, rows), rows), :]
            comb[pl.ds(pl.multiple_of((t + pad) * rows, rows), rows), :] = jnp.where(
                forward8, up, down
            )

    def by_dir(a, b):
        return jnp.where(forward8, a, b)

    zconv = [by_dir(convw_ref[0, k : k + 1, :], convw_ref[1, k : k + 1, :]) for k in range(taps)]
    zbias = by_dir(convb_ref[0:1, :], convb_ref[1:2, :])
    zdtb = by_dir(dtb_ref[0:1, :], dtb_ref[1:2, :])
    zskipw = jnp.where(lowhalf8, by_dir(skip_ref[0:1, :], skip_ref[1:2, :]), 0.0)
    chunk = 32

    @pl.loop(0, z_cells // chunk)
    def _(block):
        base = pl.multiple_of(block * (chunk * rows), chunk * rows)
        pre = zbias[None]
        for k in range(taps):
            tap = comb[pl.ds(base + k * rows, chunk * rows), :]
            pre = pre + zconv[k][None] * tap.reshape(chunk, rows, inner)
        act_b = silu(pre).reshape(chunk * rows, inner).astype(BF16)
        act = act_b.astype(F32)
        row = lax.broadcasted_iota(jnp.int32, (chunk * rows, inner), 0)
        forward = lax.rem(row, rows) < front
        low = lax.rem(row, 2) == 0
        p0 = dot_t(act_b, xwp[0])
        p1 = dot_t(act_b, xwp[1])
        proj = jnp.where(forward, p0, p1)
        s0 = jnp.dot(proj, dtwp[0], precision=lax.Precision.HIGHEST, preferred_element_type=F32)
        s1 = jnp.dot(proj, dtwp[1], precision=lax.Precision.HIGHEST, preferred_element_type=F32)
        step = jnp.where(forward, s0, s1).reshape(chunk, rows, inner) + zdtb[None]
        step = softplus(step).reshape(chunk * rows, inner)
        here = pl.ds(base, chunk * rows)
        zstep[here, :] = step
        zu[here, :] = step * act
        parts = split_lanes(jnp.where(low, proj, pltpu.roll(proj, inner - state // 2, axis=1)))
        wide = state // 2 * inner
        for g in range(2):
            zspread[here, g * wide : (g + 1) * wide] = jnp.dot(
                parts, spread[:, 2 * g * wide : (2 * g + 1) * wide], preferred_element_type=F32
            )
        zskip[here, :] = (act.reshape(chunk, rows, inner) * zskipw[None]).reshape(
            chunk * rows, inner
        )

    def lines(src_ref, ret_ref, d):
        length, pairs = src_ref.shape[0], src_ref.shape[1]
        count = 2 * pairs
        total = length * count
        both = jnp.dot(
            src_ref[...].reshape(length * pairs, 2 * width), w4[...], preferred_element_type=F32
        )
        inn[0:pad] = jnp.zeros((pad, count, inner), F32)
        inn[pad + length :] = jnp.zeros((pad, count, inner), F32)
        for par in range(2):
            part = both[:, par * inner : (par + 1) * inner].astype(BF16).astype(F32)
            inn[pad : pad + length, par * pairs : (par + 1) * pairs, :] = part.reshape(
                length, pairs, inner
            )
            gate = both[:, (2 + par) * inner : (3 + par) * inner]
            sgate[:, par * pairs : (par + 1) * pairs, :] = silu(gate).reshape(length, pairs, inner)
        for direction in range(2):
            e = d + direction
            pre = convb_ref[e : e + 1, :][None]
            for k in range(taps):
                first = k if direction == 0 else 2 * pad - k
                pre = pre + convw_ref[e, k : k + 1, :][None] * inn[first : first + length]
            act_b = silu(pre).reshape(total, inner).astype(BF16)
            act = act_b.astype(F32)
            proj = dot_t(act_b, xwp[e])
            low = jnp.dot(
                proj, dtwp[e], precision=lax.Precision.HIGHEST, preferred_element_type=F32
            )
            step = softplus(low + dtb_ref[e : e + 1, :])
            lstep[...] = step.reshape(lstep.shape)
            lu[...] = (step * act).reshape(lu.shape)
            parts = split_lanes(proj)
            for n in range(0, 2 * state, 4):
                block = slice(n * inner, (n + 4) * inner)
                lspread[:, :, block] = jnp.dot(
                    parts, spread[:, block], preferred_element_type=F32
                ).reshape(length, count, 4 * inner)
            skipped = (act * skip_ref[e : e + 1, :]).reshape(lout.shape)
            if direction == 0:
                lout[...] = skipped
            else:
                lout[...] += skipped

            @pl.loop(0, count // 8)
            def _(group):
                at = pl.ds(pl.multiple_of(group * 8, 8), 8)
                held = [jnp.zeros((8, inner), F32) for _ in range(state)]
                for i in range(length):
                    t = i if direction == 0 else length - 1 - i
                    step_t, u_t = lstep[t, at, :], lu[t, at, :]
                    result = lout[t, at, :]
                    for n in range(state):
                        inflow = u_t * lspread[t, at, n * inner : (n + 1) * inner]
                        if i == 0:
                            held[n] = inflow
                        else:
                            decay = jnp.exp2(step_t * rates[e, n : n + 1, :])
                            held[n] = decay * held[n] + inflow
                        m = state + n
                        result = result + held[n] * lspread[t, at, m * inner : (m + 1) * inner]
                    lout[t, at, :] = result

        hidden = [
            (lout[:, par * pairs : (par + 1) * pairs, :] * sgate[:, par * pairs : (par + 1) * pairs, :])
            .reshape(length * pairs, inner)
            .astype(BF16)
            for par in range(2)
        ]
        far = dot_t(jnp.concatenate(hidden, axis=1), ow2[...])
        ret_ref[...] = far.astype(BF16).reshape(ret_ref.shape)

    for y in range(y_loc):
        yin[my_col * y_loc + y] = nb[y, pl.ds(pl.multiple_of(my_col * zpy, zpy), zpy), :]
    for k in range(1, ncol):
        y_go(k).wait()
    lines(yin, yret, 2)
    for k in range(1, ncol):
        y_back(k).start()
    xin[my_row] = xs[my_row]
    for k in range(1, nrow):
        x_go(k).wait()
    lines(xin, xret, 4)
    for k in range(1, nrow):
        x_back(k).start()

    halves = state // 2
    zrate = [
        jnp.where(
            lowhalf8,
            by_dir(rates[0, n : n + 1, :], rates[1, n : n + 1, :]),
            by_dir(rates[0, halves + n : halves + n + 1, :], rates[1, halves + n : halves + n + 1, :]),
        )
        for n in range(halves)
    ]
    unroll = 8

    def advance(block, held):
        held = list(held)
        for i in range(unroll):
            t = block * unroll + i
            at = pl.ds(pl.multiple_of(t * rows, rows), rows)
            step_t, u_t = zstep[at, :], zu[at, :]
            result = zskip[at, :]
            for n in range(halves):
                decay = jnp.exp2(step_t * zrate[n])
                held[n] = decay * held[n] + u_t * zspread[at, n * inner : (n + 1) * inner]
                m = halves + n
                result = result + held[n] * zspread[at, m * inner : (m + 1) * inner]
            zout[pl.ds(pl.multiple_of(t * rows, rows), front), :] = result[0:front]
            zout[pl.ds((z_cells - 1 - t) * rows + front, front), :] = result[front:]
        return tuple(held)

    lax.fori_loop(
        0,
        z_cells // unroll,
        advance,
        tuple(jnp.zeros((rows, inner), F32) for _ in range(halves)),
    )

    near = []
    for par in range(2):
        pieces = []
        for y in range(y_loc):
            total = None
            for direction in range(2):
                for low in range(2):
                    start = par * rows + direction * front + y * 2 + low
                    part = zout[pl.ds(start, half_z, stride=2 * rows), :]
                    total = part if total is None else total + part
            pieces.append(total)
        along = jnp.concatenate(pieces, axis=0)
        near.append((along * zgate[:, par * inner : (par + 1) * inner]).astype(BF16))
    acc[...] = dot_t(jnp.concatenate(near, axis=1), ow2[...])

    yfar[my_col] = yret[pl.ds(my_col * y_loc, y_loc)]
    xfar[my_row] = xret[my_row]
    for k in range(1, ncol):
        y_back(k).wait()
    for c in range(ncol):
        for y in range(y_loc):
            acc[y * half_z + c * zpy : y * half_z + (c + 1) * zpy, :] += yfar[c, y].astype(F32)
    for k in range(1, nrow):
        x_back(k).wait()
    for r in range(nrow):
        part = xfar[r].astype(F32)
        for y in range(y_loc):
            acc[y * half_z + r * zpx : y * half_z + (r + 1) * zpx, :] += part[
                y * zpx : (y + 1) * zpx
            ]
    out_ref[...] = acc[...].astype(BF16)


def solution(mesh):
    nrow, ncol = mesh.shape["row"], mesh.shape["col"]

    def local(
        voxels,
        norm_gain,
        in_weight,
        conv_weight,
        conv_bias,
        x_weight,
        dt_weight,
        dt_bias,
        a_rate,
        skip_gain,
        out_weight,
    ):
        width = norm_gain.shape[0]
        inner = out_weight.shape[0]
        state, rank = a_rate.shape[2], dt_weight.shape[1]
        x_loc, y_loc, merged = voxels.shape
        assert x_loc == 1 and y_loc == 2
        z_cells = merged // width
        half_z = z_cells // 2
        zpy, zpx = half_z // ncol, half_z // nrow
        y_full = ncol * y_loc
        assert y_full == nrow and zpy == y_loc * zpx
        tokens = y_loc * half_z
        sizes = (nrow, ncol, y_loc, half_z, zpy, zpx, width, inner, state, rank)
        pairs = voxels.reshape(tokens, 2 * width)
        gain = norm_gain.reshape(1, width)
        line = (nrow, 2 * zpy, inner)
        zrows = 4 * y_loc * z_cells
        taps = conv_weight.shape[1]
        vmem = pl.BlockSpec(memory_space=pltpu.VMEM)
        weights = (
            in_weight,
            conv_weight,
            conv_bias,
            jnp.swapaxes(x_weight, 1, 2),
            dt_weight,
            dt_bias,
            jnp.swapaxes(a_rate, 1, 2),
            skip_gain,
            out_weight.T,
        )
        out = pl.pallas_call(
            functools.partial(kernel, sizes),
            out_shape=jax.ShapeDtypeStruct((tokens, 2 * width), BF16),
            in_specs=[vmem] * 2 + [pl.BlockSpec(memory_space=pltpu.HBM)] * 9,
            out_specs=vmem,
            scratch_shapes=[
                *[pltpu.VMEM(w.shape, w.dtype) for w in weights],
                pltpu.SemaphoreType.DMA((len(weights),)),
                pltpu.VMEM((2 * width, 4 * inner), BF16),
                pltpu.VMEM((2 * width, 2 * inner), BF16),
                pltpu.VMEM((6, 128, inner), BF16),
                pltpu.VMEM((6, 128, inner), F32),
                pltpu.VMEM((6, state, inner), F32),
                pltpu.VMEM((inner, 2 * state * inner), BF16),
                pltpu.VMEM((zrows, state * inner), F32),
                pltpu.VMEM((nrow, 2 * zpy, 2 * state * inner), F32),
                pltpu.VMEM((y_loc, half_z, 2 * width), BF16),
                pltpu.VMEM((nrow, y_loc * zpx, 2 * width), BF16),
                pltpu.VMEM((y_full, zpy, 2 * width), BF16),
                pltpu.VMEM((nrow, y_loc * zpx, 2 * width), BF16),
                pltpu.VMEM((y_full, zpy, 2 * width), BF16),
                pltpu.VMEM((nrow, y_loc * zpx, 2 * width), BF16),
                pltpu.VMEM((ncol, y_loc, zpy, 2 * width), BF16),
                pltpu.VMEM((nrow, y_loc * zpx, 2 * width), BF16),
                pltpu.VMEM((nrow + 2 * (taps - 1), 2 * zpy, inner), F32),
                pltpu.VMEM(line, F32),
                pltpu.VMEM(line, F32),
                pltpu.VMEM(line, F32),
                pltpu.VMEM(line, F32),
                pltpu.VMEM((zrows, inner), F32),
                pltpu.VMEM((zrows + (taps - 1) * 4 * y_loc, inner), F32),
                pltpu.VMEM((zrows, inner), F32),
                pltpu.VMEM((zrows, inner), F32),
                pltpu.VMEM((zrows, inner), F32),
                pltpu.VMEM((zrows, inner), F32),
                pltpu.VMEM((tokens, 2 * inner), F32),
                pltpu.VMEM((tokens, 2 * width), F32),
                pltpu.SemaphoreType.DMA((ncol,)),
                pltpu.SemaphoreType.DMA((ncol,)),
                pltpu.SemaphoreType.DMA((nrow,)),
                pltpu.SemaphoreType.DMA((nrow,)),
                pltpu.SemaphoreType.DMA((ncol,)),
                pltpu.SemaphoreType.DMA((ncol,)),
                pltpu.SemaphoreType.DMA((nrow,)),
                pltpu.SemaphoreType.DMA((nrow,)),
            ],
            compiler_params=pltpu.CompilerParams(
                collective_id=0, has_side_effects=True, vmem_limit_bytes=64 * 1024 * 1024
            ),
        )(
            pairs,
            gain,
            *weights,
        )
        return out.reshape(voxels.shape)

    in_specs = (P("row", "col", None), P(), P(), P(), P(), P(), P(), P(), P(), P(), P())
    return jax.shard_map(
        local, mesh=mesh, in_specs=in_specs, out_specs=P("row", "col", None), check_vma=False
    )
```

```python
import functools

import jax
import jax.numpy as jnp
from jax import lax
from jax.experimental import pallas as pl
from jax.experimental.pallas import tpu as pltpu
from jax.sharding import PartitionSpec as P

MESH = pl.DeviceIdType.MESH
LOG2E = 1.4426950408889634
F32 = jnp.float32
BF16 = jnp.bfloat16


def silu(x):
    half = 0.5 * x
    return half + half * jnp.tanh(half)


def softplus(x):
    u = jnp.exp(-jnp.abs(x))
    return jnp.maximum(x, 0.0) + jnp.where(u < 1e-3, u - 0.5 * u * u, jnp.log(1.0 + u))


def dot_t(a, b):
    return lax.dot_general(a, b, (((1,), (1,)), ((), ())), preferred_element_type=F32)


def split_lanes(proj):
    half = proj.shape[1] // 2
    high = proj.astype(BF16).astype(F32)
    lane = lax.broadcasted_iota(jnp.int32, proj.shape, 1)
    return jnp.where(lane < half, high, pltpu.roll(proj - high, half, axis=1)).astype(BF16)


def kernel(
    sizes,
    vox_ref,
    gain_ref,
    inw_hbm,
    convw_hbm,
    convb_hbm,
    xw_hbm,
    dtw_hbm,
    dtb_hbm,
    rate_hbm,
    skip_hbm,
    outw_hbm,
    out_ref,
    inw_ref,
    convw_ref,
    convb_ref,
    xw_ref,
    dtw_ref,
    dtb_ref,
    rate_ref,
    skip_ref,
    outw_ref,
    wsem,
    w4,
    ow2,
    xwp,
    dtwp,
    rates,
    spread,
    zspread,
    w2t,
    owd,
    cols,
    lrows,
    lhid,
    nb,
    xs,
    yin,
    xin,
    yret,
    xret,
    yfar,
    xfar,
    linn,
    lgate,
    lstep,
    lu,
    lout,
    lproj,
    zinner,
    comb,
    zstep,
    zu,
    zskip,
    zout,
    zgate,
    acc,
    ysend,
    yrecv,
    xsend,
    xrecv,
    yrsend,
    yrrecv,
    xrsend,
    xrrecv,
):
    nrow, ncol, y_loc, half_z, zpy, zpx, width, inner, state, rank = sizes
    my_row, my_col = lax.axis_index("row"), lax.axis_index("col")
    z_cells = 2 * half_z

    weights = (
        (inw_hbm, inw_ref),
        (convw_hbm, convw_ref),
        (convb_hbm, convb_ref),
        (xw_hbm, xw_ref),
        (dtw_hbm, dtw_ref),
        (dtb_hbm, dtb_ref),
        (rate_hbm, rate_ref),
        (skip_hbm, skip_ref),
        (outw_hbm, outw_ref),
    )
    fetches = [
        pltpu.make_async_copy(far, near, wsem.at[i]) for i, (far, near) in enumerate(weights)
    ]
    for fetch in fetches:
        fetch.start()
    barrier = pltpu.get_barrier_semaphore()
    for k in range(1, ncol):
        peer = lax.rem(my_col + k, ncol)
        pl.semaphore_signal(barrier, inc=1, device_id=(my_row, peer), device_id_type=MESH)
    for k in range(1, nrow):
        peer = lax.rem(my_row + k, nrow)
        pl.semaphore_signal(barrier, inc=1, device_id=(peer, my_col), device_id_type=MESH)

    values = vox_ref[...].astype(F32)
    squares = values * values
    lane = lax.broadcasted_iota(jnp.int32, values.shape, 1)
    low_half = lane < width
    mean_a = jnp.sum(jnp.where(low_half, squares, 0.0), axis=1, keepdims=True) * (1.0 / width)
    mean_b = jnp.sum(jnp.where(low_half, 0.0, squares), axis=1, keepdims=True) * (1.0 / width)
    scale = jnp.where(low_half, lax.rsqrt(mean_a + 1e-5), lax.rsqrt(mean_b + 1e-5))
    normed = values * scale * jnp.concatenate([gain_ref[...], gain_ref[...]], axis=1)
    nb[...] = normed.astype(BF16).reshape(nb.shape)
    for r in range(nrow):
        pieces = [
            normed[y * half_z + r * zpx : y * half_z + (r + 1) * zpx] for y in range(y_loc)
        ]
        xs[r] = jnp.concatenate(pieces, axis=0).astype(BF16)

    pl.semaphore_wait(barrier, ncol - 1 + nrow - 1)

    def y_go(k):
        peer = lax.rem(my_col + k, ncol)
        return pltpu.make_async_remote_copy(
            src_ref=nb.at[:, pl.ds(pl.multiple_of(peer * zpy, zpy), zpy), :],
            dst_ref=yin.at[pl.ds(my_col * y_loc, y_loc)],
            send_sem=ysend.at[k],
            recv_sem=yrecv.at[k],
            device_id=(my_row, peer),
            device_id_type=MESH,
        )

    def x_go(k):
        peer = lax.rem(my_row + k, nrow)
        return pltpu.make_async_remote_copy(
            src_ref=xs.at[peer],
            dst_ref=xin.at[my_row],
            send_sem=xsend.at[k],
            recv_sem=xrecv.at[k],
            device_id=(peer, my_col),
            device_id_type=MESH,
        )

    def y_back(k):
        peer = lax.rem(my_col + k, ncol)
        return pltpu.make_async_remote_copy(
            src_ref=yret.at[pl.ds(peer * y_loc, y_loc)],
            dst_ref=yfar.at[my_col],
            send_sem=yrsend.at[k],
            recv_sem=yrrecv.at[k],
            device_id=(my_row, peer),
            device_id_type=MESH,
        )

    def x_back(k):
        peer = lax.rem(my_row + k, nrow)
        return pltpu.make_async_remote_copy(
            src_ref=xret.at[peer],
            dst_ref=xfar.at[my_row],
            send_sem=xrsend.at[k],
            recv_sem=xrrecv.at[k],
            device_id=(peer, my_col),
            device_id_type=MESH,
        )

    for k in range(1, ncol):
        y_go(k).start()
    for k in range(1, nrow):
        x_go(k).start()

    for fetch in fetches:
        fetch.wait()
    w4[...] = jnp.zeros_like(w4)
    w4[0:width, 0:inner] = inw_ref[:, 0:inner]
    w4[width : 2 * width, inner : 2 * inner] = inw_ref[:, 0:inner]
    w4[0:width, 2 * inner : 3 * inner] = inw_ref[:, inner : 2 * inner]
    w4[width : 2 * width, 3 * inner : 4 * inner] = inw_ref[:, inner : 2 * inner]
    ow2[...] = jnp.zeros_like(ow2)
    ow2[0:width, 0:inner] = outw_ref[...]
    ow2[width : 2 * width, inner : 2 * inner] = outw_ref[...]
    xwp[...] = jnp.zeros_like(xwp)
    xwp[:, 0 : rank + 2 * state, :] = xw_ref[...]
    dtwp[...] = jnp.zeros_like(dtwp)
    dtwp[:, 0:rank, :] = dtw_ref[...]
    rates[...] = rate_ref[...] * (-LOG2E)
    w2 = jnp.concatenate([inw_ref[...], inw_ref[...]], axis=0).astype(F32)
    w2t[0:inner, :] = w2[:, 0:inner].T.astype(BF16)
    w2t[inner : 2 * inner, :] = w2[:, inner : 2 * inner].T.astype(BF16)
    owd[0:width, :] = outw_ref[...]
    owd[width : 2 * width, :] = outw_ref[...]
    taps = convw_ref.shape[1]
    proj_rows = 48
    count = cols.shape[3]
    line = lax.broadcasted_iota(jnp.int32, (128, inner), 0)
    for axis in range(2):
        d = 2 * axis + 2

        def put(at, up, down):
            cols[axis, at] = jnp.where(line < count // 2, up, down).T[:, 0:count]

        for k in range(taps):
            put(k, convw_ref[d, k : k + 1, :], convw_ref[d + 1, k : k + 1, :])
        put(taps, convb_ref[d : d + 1, :], convb_ref[d + 1 : d + 2, :])
        put(taps + 1, dtb_ref[d : d + 1, :], dtb_ref[d + 1 : d + 2, :])
        put(taps + 2, skip_ref[d : d + 1, :], skip_ref[d + 1 : d + 2, :])
        for r in range(rank):
            put(taps + 3 + r, dtw_ref[d, r : r + 1, :], dtw_ref[d + 1, r : r + 1, :])
        for n in range(state):
            put(taps + 3 + rank + n, rates[d, n : n + 1, :], rates[d + 1, n : n + 1, :])
    source = lax.broadcasted_iota(jnp.int32, (inner, inner), 0)
    for n in range(2 * state):
        hit = (source == rank + n) | (source == inner // 2 + rank + n)
        spread[:, n * inner : (n + 1) * inner] = jnp.where(hit, 1.0, 0.0).astype(BF16)

    rows = 2 * 2 * y_loc
    front = rows // 2
    row8 = lax.broadcasted_iota(jnp.int32, (rows, inner), 0)
    forward8 = row8 < front
    lowhalf8 = lax.rem(row8, 2) == 0

    full = jnp.dot(nb[...].reshape(y_loc * half_z, 2 * width), w4[...], preferred_element_type=F32)
    zgate[...] = silu(full[:, 2 * inner :])
    for par in range(2):
        own = full[:, par * inner : (par + 1) * inner].astype(BF16).astype(F32)
        for y in range(y_loc):
            piece = own[y * half_z : (y + 1) * half_z]
            for direction in range(2):
                for low in range(2):
                    start = par * rows + direction * front + y * 2 + low
                    zinner[pl.ds(start, half_z, stride=2 * rows), :] = piece
    pad = taps - 1
    comb[0 : pad * rows, :] = jnp.zeros((pad * rows, inner), F32)

    @pl.loop(0, z_cells // 8)
    def _(block):
        for i in range(8):
            t = block * 8 + i
            up = zinner[pl.ds(pl.multiple_of(t * rows, rows), rows), :]
            down = zinner[pl.ds(pl.multiple_of((z_cells - 1 - t) * rows, rows), rows), :]
            comb[pl.ds(pl.multiple_of((t + pad) * rows, rows), rows), :] = jnp.where(
                forward8, up, down
            )

    def by_dir(a, b):
        return jnp.where(forward8, a, b)

    zconv = [by_dir(convw_ref[0, k : k + 1, :], convw_ref[1, k : k + 1, :]) for k in range(taps)]
    zbias = by_dir(convb_ref[0:1, :], convb_ref[1:2, :])
    zdtb = by_dir(dtb_ref[0:1, :], dtb_ref[1:2, :])
    zskipw = jnp.where(lowhalf8, by_dir(skip_ref[0:1, :], skip_ref[1:2, :]), 0.0)
    chunk = 32

    @pl.loop(0, z_cells // chunk)
    def _(block):
        base = pl.multiple_of(block * (chunk * rows), chunk * rows)
        pre = zbias[None]
        for k in range(taps):
            tap = comb[pl.ds(base + k * rows, chunk * rows), :]
            pre = pre + zconv[k][None] * tap.reshape(chunk, rows, inner)
        act_b = silu(pre).reshape(chunk * rows, inner).astype(BF16)
        act = act_b.astype(F32)
        row = lax.broadcasted_iota(jnp.int32, (chunk * rows, inner), 0)
        forward = lax.rem(row, rows) < front
        low = lax.rem(row, 2) == 0
        p0 = dot_t(act_b, xwp[0])
        p1 = dot_t(act_b, xwp[1])
        proj = jnp.where(forward, p0, p1)
        s0 = jnp.dot(proj, dtwp[0], precision=lax.Precision.HIGHEST, preferred_element_type=F32)
        s1 = jnp.dot(proj, dtwp[1], precision=lax.Precision.HIGHEST, preferred_element_type=F32)
        step = jnp.where(forward, s0, s1).reshape(chunk, rows, inner) + zdtb[None]
        step = softplus(step).reshape(chunk * rows, inner)
        here = pl.ds(base, chunk * rows)
        zstep[here, :] = step
        zu[here, :] = step * act
        parts = split_lanes(jnp.where(low, proj, pltpu.roll(proj, inner - state // 2, axis=1)))
        wide = state // 2 * inner
        for g in range(2):
            zspread[here, g * wide : (g + 1) * wide] = jnp.dot(
                parts, spread[:, 2 * g * wide : (2 * g + 1) * wide], preferred_element_type=F32
            )
        zskip[here, :] = (act.reshape(chunk, rows, inner) * zskipw[None]).reshape(
            chunk * rows, inner
        )

    def lines(src_ref, ret_ref, d):
        length, pairs = src_ref.shape[0], src_ref.shape[1]
        count = 4 * pairs
        half = count // 2
        lane = lax.broadcasted_iota(jnp.int32, (length, pairs, 2 * width), 2)
        raw = src_ref[...].astype(F32)
        lower = jnp.where(lane < width, raw, 0.0).astype(BF16)
        upper = jnp.where(lane < width, 0.0, raw).astype(BF16)
        for t in range(length):
            back = length - 1 - t
            lrows[t, 0:pairs] = lower[t]
            lrows[t, pairs:half] = upper[t]
            lrows[t, half : half + pairs] = lower[back]
            lrows[t, half + pairs :] = upper[back]
        linn[0:pad] = jnp.zeros((pad, inner, count), F32)
        for t in range(length):
            both = dot_t(w2t[...], lrows[t])
            linn[pad + t] = both[0:inner].astype(BF16).astype(F32)
            lgate[t] = silu(both[inner:])
        upward = lax.broadcasted_iota(jnp.int32, (proj_rows, count), 1) < half
        for t in range(length):
            pre = cols[d // 2 - 1, taps]
            for k in range(taps):
                pre = pre + cols[d // 2 - 1, k] * linn[t + k]
            act_b = silu(pre).astype(BF16)
            act = act_b.astype(F32)
            p0 = jnp.dot(xwp[d, 0:proj_rows], act_b, preferred_element_type=F32)
            p1 = jnp.dot(xwp[d + 1, 0:proj_rows], act_b, preferred_element_type=F32)
            proj = jnp.where(upward, p0, p1)
            lproj[t] = proj
            low = cols[d // 2 - 1, taps + 1]
            for r in range(rank):
                low = low + cols[d // 2 - 1, taps + 3 + r] * proj[r : r + 1, :]
            step = softplus(low)
            lstep[t] = step
            lu[t] = step * act
            lout[t] = cols[d // 2 - 1, taps + 2] * act

        depth, block = 16, state // 2

        @pl.loop(0, inner // depth)
        def _(tile):
            at = pl.ds(pl.multiple_of(tile * depth, depth), depth)
            for first in range(0, state, block):
                held = [None] * block
                for t in range(length):
                    step_t, u_t, result = lstep[t, at, :], lu[t, at, :], lout[t, at, :]
                    for m in range(block):
                        n = first + m
                        inflow = u_t * lproj[t, rank + n : rank + n + 1, :]
                        if t == 0:
                            held[m] = inflow
                        else:
                            rate = cols[d // 2 - 1, taps + 3 + rank + n, at, :]
                            held[m] = jnp.exp2(step_t * rate) * held[m] + inflow
                        c = rank + state + n
                        result = result + held[m] * lproj[t, c : c + 1, :]
                    lout[t, at, :] = result

        for t in range(length):
            lhid[t] = (lout[t] * lgate[t]).T.astype(BF16)
        share = dot_t(lhid[...].reshape(length * count, inner), owd[...])
        first_half = lax.broadcasted_iota(jnp.int32, (pairs, 2 * width), 1) < width
        for t in range(length):
            start, back = t * count, (length - 1 - t) * count + half
            both = share[start : start + half] + share[back : back + half]
            ret_ref[t] = jnp.where(first_half, both[0:pairs], both[pairs:]).astype(BF16)

    for y in range(y_loc):
        yin[my_col * y_loc + y] = nb[y, pl.ds(pl.multiple_of(my_col * zpy, zpy), zpy), :]
    for k in range(1, ncol):
        y_go(k).wait()
    lines(yin, yret, 2)
    for k in range(1, ncol):
        y_back(k).start()
    xin[my_row] = xs[my_row]
    for k in range(1, nrow):
        x_go(k).wait()
    lines(xin, xret, 4)
    for k in range(1, nrow):
        x_back(k).start()

    halves = state // 2
    zrate = [
        jnp.where(
            lowhalf8,
            by_dir(rates[0, n : n + 1, :], rates[1, n : n + 1, :]),
            by_dir(rates[0, halves + n : halves + n + 1, :], rates[1, halves + n : halves + n + 1, :]),
        )
        for n in range(halves)
    ]
    unroll = 8

    def advance(block, held):
        held = list(held)
        for i in range(unroll):
            t = block * unroll + i
            at = pl.ds(pl.multiple_of(t * rows, rows), rows)
            step_t, u_t = zstep[at, :], zu[at, :]
            result = zskip[at, :]
            for n in range(halves):
                decay = jnp.exp2(step_t * zrate[n])
                held[n] = decay * held[n] + u_t * zspread[at, n * inner : (n + 1) * inner]
                m = halves + n
                result = result + held[n] * zspread[at, m * inner : (m + 1) * inner]
            zout[pl.ds(pl.multiple_of(t * rows, rows), front), :] = result[0:front]
            zout[pl.ds((z_cells - 1 - t) * rows + front, front), :] = result[front:]
        return tuple(held)

    lax.fori_loop(
        0,
        z_cells // unroll,
        advance,
        tuple(jnp.zeros((rows, inner), F32) for _ in range(halves)),
    )

    near = []
    for par in range(2):
        pieces = []
        for y in range(y_loc):
            total = None
            for direction in range(2):
                for low in range(2):
                    start = par * rows + direction * front + y * 2 + low
                    part = zout[pl.ds(start, half_z, stride=2 * rows), :]
                    total = part if total is None else total + part
            pieces.append(total)
        along = jnp.concatenate(pieces, axis=0)
        near.append((along * zgate[:, par * inner : (par + 1) * inner]).astype(BF16))
    acc[...] = dot_t(jnp.concatenate(near, axis=1), ow2[...])

    yfar[my_col] = yret[pl.ds(my_col * y_loc, y_loc)]
    xfar[my_row] = xret[my_row]
    for k in range(1, ncol):
        y_back(k).wait()
    for c in range(ncol):
        for y in range(y_loc):
            acc[y * half_z + c * zpy : y * half_z + (c + 1) * zpy, :] += yfar[c, y].astype(F32)
    for k in range(1, nrow):
        x_back(k).wait()
    for r in range(nrow):
        part = xfar[r].astype(F32)
        for y in range(y_loc):
            acc[y * half_z + r * zpx : y * half_z + (r + 1) * zpx, :] += part[
                y * zpx : (y + 1) * zpx
            ]
    out_ref[...] = acc[...].astype(BF16)


def solution(mesh):
    nrow, ncol = mesh.shape["row"], mesh.shape["col"]

    def local(
        voxels,
        norm_gain,
        in_weight,
        conv_weight,
        conv_bias,
        x_weight,
        dt_weight,
        dt_bias,
        a_rate,
        skip_gain,
        out_weight,
    ):
        width = norm_gain.shape[0]
        inner = out_weight.shape[0]
        state, rank = a_rate.shape[2], dt_weight.shape[1]
        x_loc, y_loc, merged = voxels.shape
        assert x_loc == 1 and y_loc == 2
        z_cells = merged // width
        half_z = z_cells // 2
        zpy, zpx = half_z // ncol, half_z // nrow
        y_full = ncol * y_loc
        assert y_full == nrow and zpy == y_loc * zpx
        tokens = y_loc * half_z
        sizes = (nrow, ncol, y_loc, half_z, zpy, zpx, width, inner, state, rank)
        pairs = voxels.reshape(tokens, 2 * width)
        gain = norm_gain.reshape(1, width)
        count = 4 * zpy
        line = (nrow, inner, count)
        zrows = 4 * y_loc * z_cells
        taps = conv_weight.shape[1]
        vmem = pl.BlockSpec(memory_space=pltpu.VMEM)
        weights = (
            in_weight,
            conv_weight,
            conv_bias,
            jnp.swapaxes(x_weight, 1, 2),
            dt_weight,
            dt_bias,
            jnp.swapaxes(a_rate, 1, 2),
            skip_gain,
            out_weight.T,
        )
        out = pl.pallas_call(
            functools.partial(kernel, sizes),
            out_shape=jax.ShapeDtypeStruct((tokens, 2 * width), BF16),
            in_specs=[vmem] * 2 + [pl.BlockSpec(memory_space=pltpu.HBM)] * 9,
            out_specs=vmem,
            scratch_shapes=[
                *[pltpu.VMEM(w.shape, w.dtype) for w in weights],
                pltpu.SemaphoreType.DMA((len(weights),)),
                pltpu.VMEM((2 * width, 4 * inner), BF16),
                pltpu.VMEM((2 * width, 2 * inner), BF16),
                pltpu.VMEM((6, 128, inner), BF16),
                pltpu.VMEM((6, 128, inner), F32),
                pltpu.VMEM((6, state, inner), F32),
                pltpu.VMEM((inner, 2 * state * inner), BF16),
                pltpu.VMEM((zrows, state * inner), F32),
                pltpu.VMEM((2 * inner, 2 * width), BF16),
                pltpu.VMEM((2 * width, inner), BF16),
                pltpu.VMEM((2, taps + 3 + rank + state, inner, count), F32),
                pltpu.VMEM((nrow, count, 2 * width), BF16),
                pltpu.VMEM((nrow, count, inner), BF16),
                pltpu.VMEM((y_loc, half_z, 2 * width), BF16),
                pltpu.VMEM((nrow, y_loc * zpx, 2 * width), BF16),
                pltpu.VMEM((y_full, zpy, 2 * width), BF16),
                pltpu.VMEM((nrow, y_loc * zpx, 2 * width), BF16),
                pltpu.VMEM((y_full, zpy, 2 * width), BF16),
                pltpu.VMEM((nrow, y_loc * zpx, 2 * width), BF16),
                pltpu.VMEM((ncol, y_loc, zpy, 2 * width), BF16),
                pltpu.VMEM((nrow, y_loc * zpx, 2 * width), BF16),
                pltpu.VMEM((nrow + taps - 1, inner, count), F32),
                pltpu.VMEM(line, F32),
                pltpu.VMEM(line, F32),
                pltpu.VMEM(line, F32),
                pltpu.VMEM(line, F32),
                pltpu.VMEM((nrow, 48, count), F32),
                pltpu.VMEM((zrows, inner), F32),
                pltpu.VMEM((zrows + (taps - 1) * 4 * y_loc, inner), F32),
                pltpu.VMEM((zrows, inner), F32),
                pltpu.VMEM((zrows, inner), F32),
                pltpu.VMEM((zrows, inner), F32),
                pltpu.VMEM((zrows, inner), F32),
                pltpu.VMEM((tokens, 2 * inner), F32),
                pltpu.VMEM((tokens, 2 * width), F32),
                pltpu.SemaphoreType.DMA((ncol,)),
                pltpu.SemaphoreType.DMA((ncol,)),
                pltpu.SemaphoreType.DMA((nrow,)),
                pltpu.SemaphoreType.DMA((nrow,)),
                pltpu.SemaphoreType.DMA((ncol,)),
                pltpu.SemaphoreType.DMA((ncol,)),
                pltpu.SemaphoreType.DMA((nrow,)),
                pltpu.SemaphoreType.DMA((nrow,)),
            ],
            compiler_params=pltpu.CompilerParams(
                collective_id=0, has_side_effects=True, vmem_limit_bytes=64 * 1024 * 1024
            ),
        )(
            pairs,
            gain,
            *weights,
        )
        return out.reshape(voxels.shape)

    in_specs = (P("row", "col", None), P(), P(), P(), P(), P(), P(), P(), P(), P(), P())
    return jax.shard_map(
        local, mesh=mesh, in_specs=in_specs, out_specs=P("row", "col", None), check_vma=False
    )
```

```python
import functools

import jax
import jax.numpy as jnp
from jax import lax
from jax.experimental import pallas as pl
from jax.experimental.pallas import tpu as pltpu
from jax.sharding import PartitionSpec as P

MESH = pl.DeviceIdType.MESH
LOG2E = 1.4426950408889634
F32 = jnp.float32
BF16 = jnp.bfloat16


def silu(x):
    half = 0.5 * x
    return half + half * jnp.tanh(half)


def softplus(x):
    u = jnp.exp(-jnp.abs(x))
    return jnp.maximum(x, 0.0) + jnp.where(u < 1e-3, u - 0.5 * u * u, jnp.log(1.0 + u))


def dot_t(a, b):
    return lax.dot_general(a, b, (((1,), (1,)), ((), ())), preferred_element_type=F32)


def split_lanes(proj):
    half = proj.shape[1] // 2
    high = proj.astype(BF16).astype(F32)
    lane = lax.broadcasted_iota(jnp.int32, proj.shape, 1)
    return jnp.where(lane < half, high, pltpu.roll(proj - high, half, axis=1))


def kernel(
    sizes,
    vox_ref,
    gain_ref,
    inw_hbm,
    convw_hbm,
    convb_hbm,
    xw_hbm,
    dtw_hbm,
    dtb_hbm,
    rate_hbm,
    skip_hbm,
    outw_hbm,
    out_ref,
    inw_ref,
    convw_ref,
    convb_ref,
    xw_ref,
    dtw_ref,
    dtb_ref,
    rate_ref,
    skip_ref,
    outw_ref,
    wsem,
    w4,
    ow2,
    xwp,
    dtwp,
    rates,
    spread,
    zparts,
    spread_a,
    spread_b,
    w2t,
    owd,
    cols,
    lrows,
    lhid,
    nb,
    xs,
    yin,
    xin,
    yret,
    xret,
    yfar,
    xfar,
    linn,
    lgate,
    lstep,
    lu,
    lout,
    lproj,
    zinner,
    comb,
    zstep,
    zu,
    zskip,
    zout,
    zgate,
    acc,
    ysend,
    yrecv,
    xsend,
    xrecv,
    yrsend,
    yrrecv,
    xrsend,
    xrrecv,
):
    nrow, ncol, y_loc, half_z, zpy, zpx, width, inner, state, rank = sizes
    my_row, my_col = lax.axis_index("row"), lax.axis_index("col")
    z_cells = 2 * half_z

    weights = (
        (inw_hbm, inw_ref),
        (convw_hbm, convw_ref),
        (convb_hbm, convb_ref),
        (xw_hbm, xw_ref),
        (dtw_hbm, dtw_ref),
        (dtb_hbm, dtb_ref),
        (rate_hbm, rate_ref),
        (skip_hbm, skip_ref),
        (outw_hbm, outw_ref),
    )
    fetches = [
        pltpu.make_async_copy(far, near, wsem.at[i]) for i, (far, near) in enumerate(weights)
    ]
    for fetch in fetches:
        fetch.start()
    barrier = pltpu.get_barrier_semaphore()
    for k in range(1, ncol):
        peer = lax.rem(my_col + k, ncol)
        pl.semaphore_signal(barrier, inc=1, device_id=(my_row, peer), device_id_type=MESH)
    for k in range(1, nrow):
        peer = lax.rem(my_row + k, nrow)
        pl.semaphore_signal(barrier, inc=1, device_id=(peer, my_col), device_id_type=MESH)

    @pl.loop(0, half_z // 8)
    def _(block):
        for i in range(8):
            pair = block * 8 + i
            there = pl.ds(pl.multiple_of(pair * 2 * width, 2 * width), 2 * width)
            acc[pl.ds(pair, y_loc, stride=half_z), :] = vox_ref[:, there].astype(F32)

    values = acc[...]
    squares = values * values
    lane = lax.broadcasted_iota(jnp.int32, values.shape, 1)
    low_half = lane < width
    mean_a = jnp.sum(jnp.where(low_half, squares, 0.0), axis=1, keepdims=True) * (1.0 / width)
    mean_b = jnp.sum(jnp.where(low_half, 0.0, squares), axis=1, keepdims=True) * (1.0 / width)
    scale = jnp.where(low_half, lax.rsqrt(mean_a + 1e-5), lax.rsqrt(mean_b + 1e-5))
    normed = values * scale * jnp.concatenate([gain_ref[...], gain_ref[...]], axis=1)
    nb[...] = normed.astype(BF16).reshape(nb.shape)
    for r in range(nrow):
        pieces = [
            normed[y * half_z + r * zpx : y * half_z + (r + 1) * zpx] for y in range(y_loc)
        ]
        xs[r] = jnp.concatenate(pieces, axis=0).astype(BF16)

    pl.semaphore_wait(barrier, ncol - 1 + nrow - 1)

    def y_go(k):
        peer = lax.rem(my_col + k, ncol)
        return pltpu.make_async_remote_copy(
            src_ref=nb.at[:, pl.ds(pl.multiple_of(peer * zpy, zpy), zpy), :],
            dst_ref=yin.at[pl.ds(my_col * y_loc, y_loc)],
            send_sem=ysend.at[k],
            recv_sem=yrecv.at[k],
            device_id=(my_row, peer),
            device_id_type=MESH,
        )

    def x_go(k):
        peer = lax.rem(my_row + k, nrow)
        return pltpu.make_async_remote_copy(
            src_ref=xs.at[peer],
            dst_ref=xin.at[my_row],
            send_sem=xsend.at[k],
            recv_sem=xrecv.at[k],
            device_id=(peer, my_col),
            device_id_type=MESH,
        )

    def y_back(k):
        peer = lax.rem(my_col + k, ncol)
        return pltpu.make_async_remote_copy(
            src_ref=yret.at[pl.ds(peer * y_loc, y_loc)],
            dst_ref=yfar.at[my_col],
            send_sem=yrsend.at[k],
            recv_sem=yrrecv.at[k],
            device_id=(my_row, peer),
            device_id_type=MESH,
        )

    def x_back(k):
        peer = lax.rem(my_row + k, nrow)
        return pltpu.make_async_remote_copy(
            src_ref=xret.at[peer],
            dst_ref=xfar.at[my_row],
            send_sem=xrsend.at[k],
            recv_sem=xrrecv.at[k],
            device_id=(peer, my_col),
            device_id_type=MESH,
        )

    for k in range(1, ncol):
        y_go(k).start()
    for k in range(1, nrow):
        x_go(k).start()

    for fetch in fetches:
        fetch.wait()
    w4[...] = jnp.zeros_like(w4)
    w4[0:width, 0:inner] = inw_ref[:, 0:inner]
    w4[width : 2 * width, inner : 2 * inner] = inw_ref[:, 0:inner]
    w4[0:width, 2 * inner : 3 * inner] = inw_ref[:, inner : 2 * inner]
    w4[width : 2 * width, 3 * inner : 4 * inner] = inw_ref[:, inner : 2 * inner]
    ow2[...] = jnp.zeros_like(ow2)
    ow2[0:width, 0:inner] = outw_ref[...]
    ow2[width : 2 * width, inner : 2 * inner] = outw_ref[...]
    xwp[...] = jnp.zeros_like(xwp)
    xwp[:, 0 : rank + 2 * state, :] = xw_ref[...]
    dtwp[...] = jnp.zeros_like(dtwp)
    for d in range(2):
        whole = dtw_ref[d]
        high = whole.astype(BF16)
        rest = (whole - high.astype(F32)).astype(BF16)
        for base in (0, inner // 2):
            dtwp[base : base + rank, d * inner : (d + 1) * inner] = high
            dtwp[base : base + rank, (2 + d) * inner : (3 + d) * inner] = rest
    rates[...] = rate_ref[...] * (-LOG2E)
    w2 = jnp.concatenate([inw_ref[...], inw_ref[...]], axis=0).astype(F32)
    w2t[0:inner, :] = w2[:, 0:inner].T.astype(BF16)
    w2t[inner : 2 * inner, :] = w2[:, inner : 2 * inner].T.astype(BF16)
    owd[0:width, :] = outw_ref[...]
    owd[width : 2 * width, :] = outw_ref[...]
    taps = convw_ref.shape[1]
    proj_rows = 48
    count = cols.shape[3]
    line = lax.broadcasted_iota(jnp.int32, (128, inner), 0)
    for axis in range(2):
        d = 2 * axis + 2

        def put(at, up, down):
            cols[axis, at] = jnp.where(line < count // 2, up, down).T[:, 0:count]

        for k in range(taps):
            put(k, convw_ref[d, k : k + 1, :], convw_ref[d + 1, k : k + 1, :])
        put(taps, convb_ref[d : d + 1, :], convb_ref[d + 1 : d + 2, :])
        put(taps + 1, dtb_ref[d : d + 1, :], dtb_ref[d + 1 : d + 2, :])
        put(taps + 2, skip_ref[d : d + 1, :], skip_ref[d + 1 : d + 2, :])
        for r in range(rank):
            put(taps + 3 + r, dtw_ref[d, r : r + 1, :], dtw_ref[d + 1, r : r + 1, :])
        for n in range(state):
            put(taps + 3 + rank + n, rates[d, n : n + 1, :], rates[d + 1, n : n + 1, :])
    source = lax.broadcasted_iota(jnp.int32, (inner, inner), 0)
    for n in range(2 * state):
        hit = (source == rank + n) | (source == inner // 2 + rank + n)
        spread[:, n * inner : (n + 1) * inner] = jnp.where(hit, 1.0, 0.0).astype(BF16)

    rows = 2 * 2 * y_loc
    front = rows // 2
    row8 = lax.broadcasted_iota(jnp.int32, (rows, inner), 0)
    forward8 = row8 < front
    lowhalf8 = lax.rem(row8, 2) == 0

    full = jnp.dot(nb[...].reshape(y_loc * half_z, 2 * width), w4[...], preferred_element_type=F32)
    zgate[...] = silu(full[:, 2 * inner :])
    for par in range(2):
        own = full[:, par * inner : (par + 1) * inner].astype(BF16).astype(F32)
        for y in range(y_loc):
            piece = own[y * half_z : (y + 1) * half_z]
            for direction in range(2):
                for low in range(2):
                    start = par * rows + direction * front + y * 2 + low
                    zinner[pl.ds(start, half_z, stride=2 * rows), :] = piece
    pad = taps - 1
    comb[0 : pad * rows, :] = jnp.zeros((pad * rows, inner), F32)

    @pl.loop(0, z_cells // 8)
    def _(block):
        for i in range(8):
            t = block * 8 + i
            up = zinner[pl.ds(pl.multiple_of(t * rows, rows), rows), :]
            down = zinner[pl.ds(pl.multiple_of((z_cells - 1 - t) * rows, rows), rows), :]
            comb[pl.ds(pl.multiple_of((t + pad) * rows, rows), rows), :] = jnp.where(
                forward8, up, down
            )

    def by_dir(a, b):
        return jnp.where(forward8, a, b)

    zconv = [by_dir(convw_ref[0, k : k + 1, :], convw_ref[1, k : k + 1, :]) for k in range(taps)]
    zbias = by_dir(convb_ref[0:1, :], convb_ref[1:2, :])
    zdtb = by_dir(dtb_ref[0:1, :], dtb_ref[1:2, :])
    zskipw = jnp.where(lowhalf8, by_dir(skip_ref[0:1, :], skip_ref[1:2, :]), 0.0)
    chunk = 32

    @pl.loop(0, z_cells // chunk)
    def _(block):
        base = pl.multiple_of(block * (chunk * rows), chunk * rows)
        pre = zbias[None]
        for k in range(taps):
            tap = comb[pl.ds(base + k * rows, chunk * rows), :]
            pre = pre + zconv[k][None] * tap.reshape(chunk, rows, inner)
        act_b = silu(pre).reshape(chunk * rows, inner).astype(BF16)
        act = act_b.astype(F32)
        row = lax.broadcasted_iota(jnp.int32, (chunk * rows, inner), 0)
        forward = lax.rem(row, rows) < front
        low = lax.rem(row, 2) == 0
        p0 = dot_t(act_b, xwp[0])
        p1 = dot_t(act_b, xwp[1])
        proj = jnp.where(forward, p0, p1)
        parts = split_lanes(proj)
        lowered = jnp.dot(parts.astype(BF16), dtwp[...], preferred_element_type=F32)
        s0 = lowered[:, 0:inner] + lowered[:, 2 * inner : 3 * inner]
        s1 = lowered[:, inner : 2 * inner] + lowered[:, 3 * inner : 4 * inner]
        step = jnp.where(forward, s0, s1).reshape(chunk, rows, inner) + zdtb[None]
        step = softplus(step).reshape(chunk * rows, inner)
        here = pl.ds(base, chunk * rows)
        zstep[here, :] = step
        zu[here, :] = step * act
        zparts[here, :] = jnp.where(
            low, parts, pltpu.roll(parts, inner - state // 2, axis=1)
        ).astype(BF16)
        zskip[here, :] = (act.reshape(chunk, rows, inner) * zskipw[None]).reshape(
            chunk * rows, inner
        )

    def lines(src_ref, ret_ref, d):
        length, pairs = src_ref.shape[0], src_ref.shape[1]
        count = 4 * pairs
        half = count // 2
        lane = lax.broadcasted_iota(jnp.int32, (length, pairs, 2 * width), 2)
        raw = src_ref[...].astype(F32)
        lower = jnp.where(lane < width, raw, 0.0).astype(BF16)
        upper = jnp.where(lane < width, 0.0, raw).astype(BF16)
        for t in range(length):
            back = length - 1 - t
            lrows[t, 0:pairs] = lower[t]
            lrows[t, pairs:half] = upper[t]
            lrows[t, half : half + pairs] = lower[back]
            lrows[t, half + pairs :] = upper[back]
        linn[0:pad] = jnp.zeros((pad, inner, count), F32)
        for t in range(length):
            both = dot_t(w2t[...], lrows[t])
            linn[pad + t] = both[0:inner].astype(BF16).astype(F32)
            lgate[t] = silu(both[inner:])
        upward = lax.broadcasted_iota(jnp.int32, (proj_rows, count), 1) < half
        for t in range(length):
            pre = cols[d // 2 - 1, taps]
            for k in range(taps):
                pre = pre + cols[d // 2 - 1, k] * linn[t + k]
            act_b = silu(pre).astype(BF16)
            act = act_b.astype(F32)
            p0 = jnp.dot(xwp[d, 0:proj_rows], act_b, preferred_element_type=F32)
            p1 = jnp.dot(xwp[d + 1, 0:proj_rows], act_b, preferred_element_type=F32)
            proj = jnp.where(upward, p0, p1)
            lproj[t] = proj
            low = cols[d // 2 - 1, taps + 1]
            for r in range(rank):
                low = low + cols[d // 2 - 1, taps + 3 + r] * proj[r : r + 1, :]
            step = softplus(low)
            lstep[t] = step
            lu[t] = step * act
            lout[t] = cols[d // 2 - 1, taps + 2] * act

        depth, block = 16, state // 2

        @pl.loop(0, inner // depth)
        def _(tile):
            at = pl.ds(pl.multiple_of(tile * depth, depth), depth)
            for first in range(0, state, block):
                held = [None] * block
                for t in range(length):
                    step_t, u_t, result = lstep[t, at, :], lu[t, at, :], lout[t, at, :]
                    for m in range(block):
                        n = first + m
                        inflow = u_t * lproj[t, rank + n : rank + n + 1, :]
                        if t == 0:
                            held[m] = inflow
                        else:
                            rate = cols[d // 2 - 1, taps + 3 + rank + n, at, :]
                            held[m] = jnp.exp2(step_t * rate) * held[m] + inflow
                        c = rank + state + n
                        result = result + held[m] * lproj[t, c : c + 1, :]
                    lout[t, at, :] = result

        for t in range(length):
            lhid[t] = (lout[t] * lgate[t]).T.astype(BF16)
        share = dot_t(lhid[...].reshape(length * count, inner), owd[...])
        first_half = lax.broadcasted_iota(jnp.int32, (pairs, 2 * width), 1) < width
        for t in range(length):
            start, back = t * count, (length - 1 - t) * count + half
            both = share[start : start + half] + share[back : back + half]
            ret_ref[t] = jnp.where(first_half, both[0:pairs], both[pairs:]).astype(BF16)

    for y in range(y_loc):
        yin[my_col * y_loc + y] = nb[y, pl.ds(pl.multiple_of(my_col * zpy, zpy), zpy), :]
    for k in range(1, ncol):
        y_go(k).wait()
    lines(yin, yret, 2)
    for k in range(1, ncol):
        y_back(k).start()
    xin[my_row] = xs[my_row]
    for k in range(1, nrow):
        x_go(k).wait()
    lines(xin, xret, 4)
    for k in range(1, nrow):
        x_back(k).start()

    halves = state // 2
    zrate = [
        jnp.where(
            lowhalf8,
            by_dir(rates[0, n : n + 1, :], rates[1, n : n + 1, :]),
            by_dir(rates[0, halves + n : halves + n + 1, :], rates[1, halves + n : halves + n + 1, :]),
        )
        for n in range(halves)
    ]
    wide = halves * inner
    blocks = z_cells // chunk

    def widen(block, target):
        here = pl.ds(pl.multiple_of(block * (chunk * rows), chunk * rows), chunk * rows)
        for g in range(2):
            target[:, g * wide : (g + 1) * wide] = jnp.dot(
                zparts[here, :],
                spread[:, 2 * g * wide : (2 * g + 1) * wide],
                preferred_element_type=F32,
            )

    def scan_block(block, source, held):
        for i in range(chunk):
            t = block * chunk + i
            at = pl.ds(pl.multiple_of(t * rows, rows), rows)
            step_t, u_t = zstep[at, :], zu[at, :]
            own = slice(i * rows, (i + 1) * rows)
            result = zskip[at, :]
            for n in range(halves):
                decay = jnp.exp2(step_t * zrate[n])
                held[n] = decay * held[n] + u_t * source[own, n * inner : (n + 1) * inner]
                m = halves + n
                result = result + held[n] * source[own, m * inner : (m + 1) * inner]
            zout[pl.ds(pl.multiple_of(t * rows, rows), front), :] = result[0:front]
            zout[pl.ds((z_cells - 1 - t) * rows + front, front), :] = result[front:]
        return held

    widen(0, spread_a)

    def advance(pair, held):
        held = list(held)
        widen(2 * pair + 1, spread_b)
        held = scan_block(2 * pair, spread_a, held)
        widen(lax.rem(2 * pair + 2, blocks), spread_a)
        held = scan_block(2 * pair + 1, spread_b, held)
        return tuple(held)

    lax.fori_loop(
        0,
        blocks // 2,
        advance,
        tuple(jnp.zeros((rows, inner), F32) for _ in range(halves)),
    )

    near = []
    for par in range(2):
        pieces = []
        for y in range(y_loc):
            total = None
            for direction in range(2):
                for low in range(2):
                    start = par * rows + direction * front + y * 2 + low
                    part = zout[pl.ds(start, half_z, stride=2 * rows), :]
                    total = part if total is None else total + part
            pieces.append(total)
        along = jnp.concatenate(pieces, axis=0)
        near.append((along * zgate[:, par * inner : (par + 1) * inner]).astype(BF16))
    acc[...] = dot_t(jnp.concatenate(near, axis=1), ow2[...])

    yfar[my_col] = yret[pl.ds(my_col * y_loc, y_loc)]
    xfar[my_row] = xret[my_row]
    for k in range(1, ncol):
        y_back(k).wait()
    for c in range(ncol):
        for y in range(y_loc):
            acc[y * half_z + c * zpy : y * half_z + (c + 1) * zpy, :] += yfar[c, y].astype(F32)
    for k in range(1, nrow):
        x_back(k).wait()
    for r in range(nrow):
        part = xfar[r].astype(F32)
        for y in range(y_loc):
            acc[y * half_z + r * zpx : y * half_z + (r + 1) * zpx, :] += part[
                y * zpx : (y + 1) * zpx
            ]

    @pl.loop(0, half_z // 8)
    def _(block):
        for i in range(8):
            pair = block * 8 + i
            there = pl.ds(pl.multiple_of(pair * 2 * width, 2 * width), 2 * width)
            out_ref[:, there] = acc[pl.ds(pair, y_loc, stride=half_z), :].astype(BF16)


def solution(mesh):
    nrow, ncol = mesh.shape["row"], mesh.shape["col"]

    def local(
        voxels,
        norm_gain,
        in_weight,
        conv_weight,
        conv_bias,
        x_weight,
        dt_weight,
        dt_bias,
        a_rate,
        skip_gain,
        out_weight,
    ):
        width = norm_gain.shape[0]
        inner = out_weight.shape[0]
        state, rank = a_rate.shape[2], dt_weight.shape[1]
        x_loc, y_loc, merged = voxels.shape
        assert x_loc == 1 and y_loc == 2
        z_cells = merged // width
        half_z = z_cells // 2
        zpy, zpx = half_z // ncol, half_z // nrow
        y_full = ncol * y_loc
        assert y_full == nrow and zpy == y_loc * zpx
        tokens = y_loc * half_z
        sizes = (nrow, ncol, y_loc, half_z, zpy, zpx, width, inner, state, rank)
        pairs = voxels.reshape(y_loc, merged)
        gain = norm_gain.reshape(1, width)
        count = 4 * zpy
        line = (nrow, inner, count)
        zrows = 4 * y_loc * z_cells
        taps = conv_weight.shape[1]
        vmem = pl.BlockSpec(memory_space=pltpu.VMEM)
        weights = (
            in_weight,
            conv_weight,
            conv_bias,
            jnp.swapaxes(x_weight, 1, 2),
            dt_weight,
            dt_bias,
            jnp.swapaxes(a_rate, 1, 2),
            skip_gain,
            out_weight.T,
        )
        out = pl.pallas_call(
            functools.partial(kernel, sizes),
            out_shape=jax.ShapeDtypeStruct((y_loc, merged), BF16),
            in_specs=[vmem] * 2 + [pl.BlockSpec(memory_space=pltpu.HBM)] * 9,
            out_specs=vmem,
            scratch_shapes=[
                *[pltpu.VMEM(w.shape, w.dtype) for w in weights],
                pltpu.SemaphoreType.DMA((len(weights),)),
                pltpu.VMEM((2 * width, 4 * inner), BF16),
                pltpu.VMEM((2 * width, 2 * inner), BF16),
                pltpu.VMEM((6, 128, inner), BF16),
                pltpu.VMEM((inner, 4 * inner), BF16),
                pltpu.VMEM((6, state, inner), F32),
                pltpu.VMEM((inner, 2 * state * inner), BF16),
                pltpu.VMEM((zrows, inner), BF16),
                pltpu.VMEM((32 * 4 * y_loc, state * inner), F32),
                pltpu.VMEM((32 * 4 * y_loc, state * inner), F32),
                pltpu.VMEM((2 * inner, 2 * width), BF16),
                pltpu.VMEM((2 * width, inner), BF16),
                pltpu.VMEM((2, taps + 3 + rank + state, inner, count), F32),
                pltpu.VMEM((nrow, count, 2 * width), BF16),
                pltpu.VMEM((nrow, count, inner), BF16),
                pltpu.VMEM((y_loc, half_z, 2 * width), BF16),
                pltpu.VMEM((nrow, y_loc * zpx, 2 * width), BF16),
                pltpu.VMEM((y_full, zpy, 2 * width), BF16),
                pltpu.VMEM((nrow, y_loc * zpx, 2 * width), BF16),
                pltpu.VMEM((y_full, zpy, 2 * width), BF16),
                pltpu.VMEM((nrow, y_loc * zpx, 2 * width), BF16),
                pltpu.VMEM((ncol, y_loc, zpy, 2 * width), BF16),
                pltpu.VMEM((nrow, y_loc * zpx, 2 * width), BF16),
                pltpu.VMEM((nrow + taps - 1, inner, count), F32),
                pltpu.VMEM(line, F32),
                pltpu.VMEM(line, F32),
                pltpu.VMEM(line, F32),
                pltpu.VMEM(line, F32),
                pltpu.VMEM((nrow, 48, count), F32),
                pltpu.VMEM((zrows, inner), F32),
                pltpu.VMEM((zrows + (taps - 1) * 4 * y_loc, inner), F32),
                pltpu.VMEM((zrows, inner), F32),
                pltpu.VMEM((zrows, inner), F32),
                pltpu.VMEM((zrows, inner), F32),
                pltpu.VMEM((zrows, inner), F32),
                pltpu.VMEM((tokens, 2 * inner), F32),
                pltpu.VMEM((tokens, 2 * width), F32),
                pltpu.SemaphoreType.DMA((ncol,)),
                pltpu.SemaphoreType.DMA((ncol,)),
                pltpu.SemaphoreType.DMA((nrow,)),
                pltpu.SemaphoreType.DMA((nrow,)),
                pltpu.SemaphoreType.DMA((ncol,)),
                pltpu.SemaphoreType.DMA((ncol,)),
                pltpu.SemaphoreType.DMA((nrow,)),
                pltpu.SemaphoreType.DMA((nrow,)),
            ],
            compiler_params=pltpu.CompilerParams(
                collective_id=0, has_side_effects=True, vmem_limit_bytes=64 * 1024 * 1024
            ),
        )(
            pairs,
            gain,
            *weights,
        )
        return out.reshape(voxels.shape)

    in_specs = (P("row", "col", None), P(), P(), P(), P(), P(), P(), P(), P(), P(), P())
    return jax.shard_map(
        local, mesh=mesh, in_specs=in_specs, out_specs=P("row", "col", None), check_vma=False
    )
```

```python
import functools

import jax
import jax.numpy as jnp
from jax import lax
from jax.experimental import pallas as pl
from jax.experimental.pallas import tpu as pltpu
from jax.sharding import PartitionSpec as P

MESH = pl.DeviceIdType.MESH
LOG2E = 1.4426950408889634
F32 = jnp.float32
BF16 = jnp.bfloat16


def silu(x):
    half = 0.5 * x
    return half + half * jnp.tanh(half)


def softplus(x):
    u = jnp.exp(-jnp.abs(x))
    return jnp.maximum(x, 0.0) + jnp.where(u < 1e-3, u - 0.5 * u * u, jnp.log(1.0 + u))


def dot_t(a, b):
    return lax.dot_general(a, b, (((1,), (1,)), ((), ())), preferred_element_type=F32)


def split_lanes(proj):
    half = proj.shape[1] // 2
    high = proj.astype(BF16).astype(F32)
    lane = lax.broadcasted_iota(jnp.int32, proj.shape, 1)
    return jnp.where(lane < half, high, pltpu.roll(proj - high, half, axis=1))


def kernel(
    sizes,
    vox_hbm,
    gain_hbm,
    inw_hbm,
    convw_hbm,
    convb_hbm,
    xw_hbm,
    dtw_hbm,
    dtb_hbm,
    rate_hbm,
    skip_hbm,
    outw_hbm,
    out_ref,
    vox_ref,
    gain_ref,
    inw_ref,
    convw_ref,
    convb_ref,
    xw_ref,
    dtw_ref,
    dtb_ref,
    rate_ref,
    skip_ref,
    outw_ref,
    wsem,
    w4,
    ow2,
    xwp,
    dtwp,
    rates,
    spread,
    zparts,
    spread_a,
    spread_b,
    w2t,
    owd,
    cols,
    lrows,
    lhid,
    nb,
    xs,
    yin,
    xin,
    yret,
    xret,
    yfar,
    xfar,
    linn,
    lgate,
    lstep,
    lu,
    lout,
    lproj,
    zinner,
    comb,
    zstep,
    zu,
    zskip,
    zout,
    zgate,
    acc,
    ysend,
    yrecv,
    xsend,
    xrecv,
    yrsend,
    yrrecv,
    xrsend,
    xrrecv,
):
    nrow, ncol, y_loc, half_z, zpy, zpx, width, inner, state, rank = sizes
    my_row, my_col = lax.axis_index("row"), lax.axis_index("col")
    z_cells = 2 * half_z

    weights = (
        (vox_hbm, vox_ref),
        (gain_hbm, gain_ref),
        (inw_hbm, inw_ref),
        (convw_hbm, convw_ref),
        (convb_hbm, convb_ref),
        (xw_hbm, xw_ref),
        (dtw_hbm, dtw_ref),
        (dtb_hbm, dtb_ref),
        (rate_hbm, rate_ref),
        (skip_hbm, skip_ref),
        (outw_hbm, outw_ref),
    )
    fetches = [
        pltpu.make_async_copy(far, near, wsem.at[i]) for i, (far, near) in enumerate(weights)
    ]
    for fetch in fetches:
        fetch.start()
    barrier = pltpu.get_barrier_semaphore()
    for k in range(1, ncol):
        peer = lax.rem(my_col + k, ncol)
        pl.semaphore_signal(barrier, inc=1, device_id=(my_row, peer), device_id_type=MESH)
    for k in range(1, nrow):
        peer = lax.rem(my_row + k, nrow)
        pl.semaphore_signal(barrier, inc=1, device_id=(peer, my_col), device_id_type=MESH)

    for fetch in fetches[:2]:
        fetch.wait()

    @pl.loop(0, half_z // 8)
    def _(block):
        for i in range(8):
            pair = block * 8 + i
            there = pl.ds(pl.multiple_of(pair * 2 * width, 2 * width), 2 * width)
            acc[pl.ds(pair, y_loc, stride=half_z), :] = vox_ref[:, there].astype(F32)

    values = acc[...]
    squares = values * values
    lane = lax.broadcasted_iota(jnp.int32, values.shape, 1)
    low_half = lane < width
    mean_a = jnp.sum(jnp.where(low_half, squares, 0.0), axis=1, keepdims=True) * (1.0 / width)
    mean_b = jnp.sum(jnp.where(low_half, 0.0, squares), axis=1, keepdims=True) * (1.0 / width)
    scale = jnp.where(low_half, lax.rsqrt(mean_a + 1e-5), lax.rsqrt(mean_b + 1e-5))
    normed = values * scale * jnp.concatenate([gain_ref[...], gain_ref[...]], axis=1)
    nb[...] = normed.astype(BF16).reshape(nb.shape)
    for r in range(nrow):
        pieces = [
            normed[y * half_z + r * zpx : y * half_z + (r + 1) * zpx] for y in range(y_loc)
        ]
        xs[r] = jnp.concatenate(pieces, axis=0).astype(BF16)

    pl.semaphore_wait(barrier, ncol - 1 + nrow - 1)

    def y_go(k):
        peer = lax.rem(my_col + k, ncol)
        return pltpu.make_async_remote_copy(
            src_ref=nb.at[:, pl.ds(pl.multiple_of(peer * zpy, zpy), zpy), :],
            dst_ref=yin.at[pl.ds(my_col * y_loc, y_loc)],
            send_sem=ysend.at[k],
            recv_sem=yrecv.at[k],
            device_id=(my_row, peer),
            device_id_type=MESH,
        )

    def x_go(k):
        peer = lax.rem(my_row + k, nrow)
        return pltpu.make_async_remote_copy(
            src_ref=xs.at[peer],
            dst_ref=xin.at[my_row],
            send_sem=xsend.at[k],
            recv_sem=xrecv.at[k],
            device_id=(peer, my_col),
            device_id_type=MESH,
        )

    def y_back(k):
        peer = lax.rem(my_col + k, ncol)
        return pltpu.make_async_remote_copy(
            src_ref=yret.at[pl.ds(peer * y_loc, y_loc)],
            dst_ref=yfar.at[my_col],
            send_sem=yrsend.at[k],
            recv_sem=yrrecv.at[k],
            device_id=(my_row, peer),
            device_id_type=MESH,
        )

    def x_back(k):
        peer = lax.rem(my_row + k, nrow)
        return pltpu.make_async_remote_copy(
            src_ref=xret.at[peer],
            dst_ref=xfar.at[my_row],
            send_sem=xrsend.at[k],
            recv_sem=xrrecv.at[k],
            device_id=(peer, my_col),
            device_id_type=MESH,
        )

    for k in range(1, ncol):
        y_go(k).start()
    for k in range(1, nrow):
        x_go(k).start()

    for fetch in fetches[2:]:
        fetch.wait()
    w4[...] = jnp.zeros_like(w4)
    w4[0:width, 0:inner] = inw_ref[:, 0:inner]
    w4[width : 2 * width, inner : 2 * inner] = inw_ref[:, 0:inner]
    w4[0:width, 2 * inner : 3 * inner] = inw_ref[:, inner : 2 * inner]
    w4[width : 2 * width, 3 * inner : 4 * inner] = inw_ref[:, inner : 2 * inner]
    ow2[...] = jnp.zeros_like(ow2)
    ow2[0:width, 0:inner] = outw_ref[...]
    ow2[width : 2 * width, inner : 2 * inner] = outw_ref[...]
    xwp[...] = jnp.zeros_like(xwp)
    xwp[:, 0 : rank + 2 * state, :] = xw_ref[...]
    dtwp[...] = jnp.zeros_like(dtwp)
    for d in range(2):
        whole = dtw_ref[d]
        high = whole.astype(BF16)
        rest = (whole - high.astype(F32)).astype(BF16)
        for base in (0, inner // 2):
            dtwp[base : base + rank, d * inner : (d + 1) * inner] = high
            dtwp[base : base + rank, (2 + d) * inner : (3 + d) * inner] = rest
    rates[...] = rate_ref[...] * (-LOG2E)
    w2 = jnp.concatenate([inw_ref[...], inw_ref[...]], axis=0).astype(F32)
    w2t[0:inner, :] = w2[:, 0:inner].T.astype(BF16)
    w2t[inner : 2 * inner, :] = w2[:, inner : 2 * inner].T.astype(BF16)
    owd[0:width, :] = outw_ref[...]
    owd[width : 2 * width, :] = outw_ref[...]
    taps = convw_ref.shape[1]
    proj_rows = 48
    count = cols.shape[3]
    line = lax.broadcasted_iota(jnp.int32, (128, inner), 0)
    for axis in range(2):
        d = 2 * axis + 2

        def put(at, up, down):
            cols[axis, at] = jnp.where(line < count // 2, up, down).T[:, 0:count]

        for k in range(taps):
            put(k, convw_ref[d, k : k + 1, :], convw_ref[d + 1, k : k + 1, :])
        put(taps, convb_ref[d : d + 1, :], convb_ref[d + 1 : d + 2, :])
        put(taps + 1, dtb_ref[d : d + 1, :], dtb_ref[d + 1 : d + 2, :])
        put(taps + 2, skip_ref[d : d + 1, :], skip_ref[d + 1 : d + 2, :])
        for r in range(rank):
            put(taps + 3 + r, dtw_ref[d, r : r + 1, :], dtw_ref[d + 1, r : r + 1, :])
        for n in range(state):
            put(taps + 3 + rank + n, rates[d, n : n + 1, :], rates[d + 1, n : n + 1, :])
    source = lax.broadcasted_iota(jnp.int32, (inner, inner), 0)
    for n in range(2 * state):
        hit = (source == rank + n) | (source == inner // 2 + rank + n)
        spread[:, n * inner : (n + 1) * inner] = jnp.where(hit, 1.0, 0.0).astype(BF16)

    rows = 2 * 2 * y_loc
    front = rows // 2
    row8 = lax.broadcasted_iota(jnp.int32, (rows, inner), 0)
    forward8 = row8 < front
    lowhalf8 = lax.rem(row8, 2) == 0

    full = jnp.dot(nb[...].reshape(y_loc * half_z, 2 * width), w4[...], preferred_element_type=F32)
    zgate[...] = silu(full[:, 2 * inner :])
    for par in range(2):
        own = full[:, par * inner : (par + 1) * inner].astype(BF16).astype(F32)
        for y in range(y_loc):
            piece = own[y * half_z : (y + 1) * half_z]
            for direction in range(2):
                for low in range(2):
                    start = par * rows + direction * front + y * 2 + low
                    zinner[pl.ds(start, half_z, stride=2 * rows), :] = piece
    pad = taps - 1
    comb[0 : pad * rows, :] = jnp.zeros((pad * rows, inner), F32)

    @pl.loop(0, z_cells // 8)
    def _(block):
        for i in range(8):
            t = block * 8 + i
            up = zinner[pl.ds(pl.multiple_of(t * rows, rows), rows), :]
            down = zinner[pl.ds(pl.multiple_of((z_cells - 1 - t) * rows, rows), rows), :]
            comb[pl.ds(pl.multiple_of((t + pad) * rows, rows), rows), :] = jnp.where(
                forward8, up, down
            )

    def by_dir(a, b):
        return jnp.where(forward8, a, b)

    zconv = [by_dir(convw_ref[0, k : k + 1, :], convw_ref[1, k : k + 1, :]) for k in range(taps)]
    zbias = by_dir(convb_ref[0:1, :], convb_ref[1:2, :])
    zdtb = by_dir(dtb_ref[0:1, :], dtb_ref[1:2, :])
    zskipw = jnp.where(lowhalf8, by_dir(skip_ref[0:1, :], skip_ref[1:2, :]), 0.0)
    chunk = 32

    large = z_cells // 2

    @pl.loop(0, z_cells // large)
    def _(block):
        base = pl.multiple_of(block * (large * rows), large * rows)
        pre = zbias[None]
        for k in range(taps):
            tap = comb[pl.ds(base + k * rows, large * rows), :]
            pre = pre + zconv[k][None] * tap.reshape(large, rows, inner)
        act_b = silu(pre).reshape(large * rows, inner).astype(BF16)
        act = act_b.astype(F32)
        row = lax.broadcasted_iota(jnp.int32, (large * rows, inner), 0)
        forward = lax.rem(row, rows) < front
        low = lax.rem(row, 2) == 0
        either = dot_t(act_b, xwp[0:2].reshape(2 * inner, inner))
        proj = jnp.where(forward, either[:, 0:inner], either[:, inner:])
        parts = split_lanes(proj)
        lowered = jnp.dot(parts.astype(BF16), dtwp[...], preferred_element_type=F32)
        s0 = lowered[:, 0:inner] + lowered[:, 2 * inner : 3 * inner]
        s1 = lowered[:, inner : 2 * inner] + lowered[:, 3 * inner : 4 * inner]
        step = jnp.where(forward, s0, s1).reshape(large, rows, inner) + zdtb[None]
        step = softplus(step).reshape(large * rows, inner)
        here = pl.ds(base, large * rows)
        zstep[here, :] = step
        zu[here, :] = step * act
        zparts[here, :] = jnp.where(
            low, parts, pltpu.roll(parts, inner - state // 2, axis=1)
        ).astype(BF16)
        zskip[here, :] = (act.reshape(large, rows, inner) * zskipw[None]).reshape(
            large * rows, inner
        )

    def lines(src_ref, ret_ref, d):
        length, pairs = src_ref.shape[0], src_ref.shape[1]
        count = 4 * pairs
        half = count // 2
        lane = lax.broadcasted_iota(jnp.int32, (length, pairs, 2 * width), 2)
        raw = src_ref[...].astype(F32)
        lower = jnp.where(lane < width, raw, 0.0).astype(BF16)
        upper = jnp.where(lane < width, 0.0, raw).astype(BF16)
        for t in range(length):
            back = length - 1 - t
            lrows[t, 0:pairs] = lower[t]
            lrows[t, pairs:half] = upper[t]
            lrows[t, half : half + pairs] = lower[back]
            lrows[t, half + pairs :] = upper[back]
        linn[0:pad] = jnp.zeros((pad, inner, count), F32)
        for t in range(length):
            both = dot_t(w2t[...], lrows[t])
            linn[pad + t] = both[0:inner].astype(BF16).astype(F32)
            lgate[t] = silu(both[inner:])
        x_maps = jnp.concatenate([xwp[d, 0:proj_rows], xwp[d + 1, 0:proj_rows]], axis=0)
        upward = lax.broadcasted_iota(jnp.int32, (proj_rows, count), 1) < half
        for t in range(length):
            pre = cols[d // 2 - 1, taps]
            for k in range(taps):
                pre = pre + cols[d // 2 - 1, k] * linn[t + k]
            act_b = silu(pre).astype(BF16)
            act = act_b.astype(F32)
            either = jnp.dot(x_maps, act_b, preferred_element_type=F32)
            proj = jnp.where(upward, either[0:proj_rows], either[proj_rows:])
            lproj[t] = proj
            low = cols[d // 2 - 1, taps + 1]
            for r in range(rank):
                low = low + cols[d // 2 - 1, taps + 3 + r] * proj[r : r + 1, :]
            step = softplus(low)
            lstep[t] = step
            lu[t] = step * act
            lout[t] = cols[d // 2 - 1, taps + 2] * act

        depth, block = 16, state // 2

        @pl.loop(0, inner // depth)
        def _(tile):
            at = pl.ds(pl.multiple_of(tile * depth, depth), depth)
            for first in range(0, state, block):
                held = [None] * block
                for t in range(length):
                    step_t, u_t, result = lstep[t, at, :], lu[t, at, :], lout[t, at, :]
                    for m in range(block):
                        n = first + m
                        inflow = u_t * lproj[t, rank + n : rank + n + 1, :]
                        if t == 0:
                            held[m] = inflow
                        else:
                            rate = cols[d // 2 - 1, taps + 3 + rank + n, at, :]
                            held[m] = jnp.exp2(step_t * rate) * held[m] + inflow
                        c = rank + state + n
                        result = result + held[m] * lproj[t, c : c + 1, :]
                    lout[t, at, :] = result

        for t in range(length):
            lhid[t] = (lout[t] * lgate[t]).T.astype(BF16)
        share = dot_t(lhid[...].reshape(length * count, inner), owd[...])
        first_half = lax.broadcasted_iota(jnp.int32, (pairs, 2 * width), 1) < width
        for t in range(length):
            start, back = t * count, (length - 1 - t) * count + half
            both = share[start : start + half] + share[back : back + half]
            ret_ref[t] = jnp.where(first_half, both[0:pairs], both[pairs:]).astype(BF16)

    for y in range(y_loc):
        yin[my_col * y_loc + y] = nb[y, pl.ds(pl.multiple_of(my_col * zpy, zpy), zpy), :]
    for k in range(1, ncol):
        y_go(k).wait()
    lines(yin, yret, 2)
    for k in range(1, ncol):
        y_back(k).start()
    xin[my_row] = xs[my_row]
    for k in range(1, nrow):
        x_go(k).wait()
    lines(xin, xret, 4)
    for k in range(1, nrow):
        x_back(k).start()

    halves = state // 2
    zrate = [
        jnp.where(
            lowhalf8,
            by_dir(rates[0, n : n + 1, :], rates[1, n : n + 1, :]),
            by_dir(rates[0, halves + n : halves + n + 1, :], rates[1, halves + n : halves + n + 1, :]),
        )
        for n in range(halves)
    ]
    wide = halves * inner
    blocks = z_cells // chunk

    def widen(block, target):
        here = pl.ds(pl.multiple_of(block * (chunk * rows), chunk * rows), chunk * rows)
        for g in range(2):
            target[:, g * wide : (g + 1) * wide] = jnp.dot(
                zparts[here, :],
                spread[:, 2 * g * wide : (2 * g + 1) * wide],
                preferred_element_type=F32,
            )

    def scan_block(block, source, held):
        for i in range(chunk):
            t = block * chunk + i
            at = pl.ds(pl.multiple_of(t * rows, rows), rows)
            step_t, u_t = zstep[at, :], zu[at, :]
            own = slice(i * rows, (i + 1) * rows)
            result = zskip[at, :]
            for n in range(halves):
                decay = jnp.exp2(step_t * zrate[n])
                held[n] = decay * held[n] + u_t * source[own, n * inner : (n + 1) * inner]
                m = halves + n
                result = result + held[n] * source[own, m * inner : (m + 1) * inner]
            zout[pl.ds(pl.multiple_of(t * rows, rows), front), :] = result[0:front]
            zout[pl.ds((z_cells - 1 - t) * rows + front, front), :] = result[front:]
        return held

    widen(0, spread_a)

    def advance(pair, held):
        held = list(held)
        widen(2 * pair + 1, spread_b)
        held = scan_block(2 * pair, spread_a, held)
        widen(lax.rem(2 * pair + 2, blocks), spread_a)
        held = scan_block(2 * pair + 1, spread_b, held)
        return tuple(held)

    lax.fori_loop(
        0,
        blocks // 2,
        advance,
        tuple(jnp.zeros((rows, inner), F32) for _ in range(halves)),
    )

    near = []
    for par in range(2):
        pieces = []
        for y in range(y_loc):
            total = None
            for direction in range(2):
                for low in range(2):
                    start = par * rows + direction * front + y * 2 + low
                    part = zout[pl.ds(start, half_z, stride=2 * rows), :]
                    total = part if total is None else total + part
            pieces.append(total)
        along = jnp.concatenate(pieces, axis=0)
        near.append((along * zgate[:, par * inner : (par + 1) * inner]).astype(BF16))
    acc[...] = dot_t(jnp.concatenate(near, axis=1), ow2[...])

    yfar[my_col] = yret[pl.ds(my_col * y_loc, y_loc)]
    xfar[my_row] = xret[my_row]
    for k in range(1, ncol):
        y_back(k).wait()
    for c in range(ncol):
        for y in range(y_loc):
            acc[y * half_z + c * zpy : y * half_z + (c + 1) * zpy, :] += yfar[c, y].astype(F32)
    for k in range(1, nrow):
        x_back(k).wait()
    for r in range(nrow):
        part = xfar[r].astype(F32)
        for y in range(y_loc):
            acc[y * half_z + r * zpx : y * half_z + (r + 1) * zpx, :] += part[
                y * zpx : (y + 1) * zpx
            ]

    @pl.loop(0, half_z // 8)
    def _(block):
        for i in range(8):
            pair = block * 8 + i
            there = pl.ds(pl.multiple_of(pair * 2 * width, 2 * width), 2 * width)
            out_ref[:, there] = acc[pl.ds(pair, y_loc, stride=half_z), :].astype(BF16)


def solution(mesh):
    nrow, ncol = mesh.shape["row"], mesh.shape["col"]

    def local(
        voxels,
        norm_gain,
        in_weight,
        conv_weight,
        conv_bias,
        x_weight,
        dt_weight,
        dt_bias,
        a_rate,
        skip_gain,
        out_weight,
    ):
        width = norm_gain.shape[0]
        inner = out_weight.shape[0]
        state, rank = a_rate.shape[2], dt_weight.shape[1]
        x_loc, y_loc, merged = voxels.shape
        assert x_loc == 1 and y_loc == 2
        z_cells = merged // width
        half_z = z_cells // 2
        zpy, zpx = half_z // ncol, half_z // nrow
        y_full = ncol * y_loc
        assert y_full == nrow and zpy == y_loc * zpx
        tokens = y_loc * half_z
        sizes = (nrow, ncol, y_loc, half_z, zpy, zpx, width, inner, state, rank)
        pairs = voxels.reshape(y_loc, merged)
        gain = norm_gain.reshape(1, width)
        count = 4 * zpy
        line = (nrow, inner, count)
        zrows = 4 * y_loc * z_cells
        taps = conv_weight.shape[1]
        vmem = pl.BlockSpec(memory_space=pltpu.VMEM)
        operands = (
            pairs,
            gain,
            in_weight,
            conv_weight,
            conv_bias,
            jnp.swapaxes(x_weight, 1, 2),
            dt_weight,
            dt_bias,
            jnp.swapaxes(a_rate, 1, 2),
            skip_gain,
            out_weight.T,
        )
        out = pl.pallas_call(
            functools.partial(kernel, sizes),
            out_shape=jax.ShapeDtypeStruct((y_loc, merged), BF16),
            in_specs=[pl.BlockSpec(memory_space=pltpu.HBM)] * len(operands),
            out_specs=vmem,
            scratch_shapes=[
                *[pltpu.VMEM(w.shape, w.dtype) for w in operands],
                pltpu.SemaphoreType.DMA((len(operands),)),
                pltpu.VMEM((2 * width, 4 * inner), BF16),
                pltpu.VMEM((2 * width, 2 * inner), BF16),
                pltpu.VMEM((6, 128, inner), BF16),
                pltpu.VMEM((inner, 4 * inner), BF16),
                pltpu.VMEM((6, state, inner), F32),
                pltpu.VMEM((inner, 2 * state * inner), BF16),
                pltpu.VMEM((zrows, inner), BF16),
                pltpu.VMEM((32 * 4 * y_loc, state * inner), F32),
                pltpu.VMEM((32 * 4 * y_loc, state * inner), F32),
                pltpu.VMEM((2 * inner, 2 * width), BF16),
                pltpu.VMEM((2 * width, inner), BF16),
                pltpu.VMEM((2, taps + 3 + rank + state, inner, count), F32),
                pltpu.VMEM((nrow, count, 2 * width), BF16),
                pltpu.VMEM((nrow, count, inner), BF16),
                pltpu.VMEM((y_loc, half_z, 2 * width), BF16),
                pltpu.VMEM((nrow, y_loc * zpx, 2 * width), BF16),
                pltpu.VMEM((y_full, zpy, 2 * width), BF16),
                pltpu.VMEM((nrow, y_loc * zpx, 2 * width), BF16),
                pltpu.VMEM((y_full, zpy, 2 * width), BF16),
                pltpu.VMEM((nrow, y_loc * zpx, 2 * width), BF16),
                pltpu.VMEM((ncol, y_loc, zpy, 2 * width), BF16),
                pltpu.VMEM((nrow, y_loc * zpx, 2 * width), BF16),
                pltpu.VMEM((nrow + taps - 1, inner, count), F32),
                pltpu.VMEM(line, F32),
                pltpu.VMEM(line, F32),
                pltpu.VMEM(line, F32),
                pltpu.VMEM(line, F32),
                pltpu.VMEM((nrow, 48, count), F32),
                pltpu.VMEM((zrows, inner), F32),
                pltpu.VMEM((zrows + (taps - 1) * 4 * y_loc, inner), F32),
                pltpu.VMEM((zrows, inner), F32),
                pltpu.VMEM((zrows, inner), F32),
                pltpu.VMEM((zrows, inner), F32),
                pltpu.VMEM((zrows, inner), F32),
                pltpu.VMEM((tokens, 2 * inner), F32),
                pltpu.VMEM((tokens, 2 * width), F32),
                pltpu.SemaphoreType.DMA((ncol,)),
                pltpu.SemaphoreType.DMA((ncol,)),
                pltpu.SemaphoreType.DMA((nrow,)),
                pltpu.SemaphoreType.DMA((nrow,)),
                pltpu.SemaphoreType.DMA((ncol,)),
                pltpu.SemaphoreType.DMA((ncol,)),
                pltpu.SemaphoreType.DMA((nrow,)),
                pltpu.SemaphoreType.DMA((nrow,)),
            ],
            compiler_params=pltpu.CompilerParams(
                collective_id=0, has_side_effects=True, vmem_limit_bytes=64 * 1024 * 1024
            ),
        )(
            *operands,
        )
        return out.reshape(voxels.shape)

    in_specs = (P("row", "col", None), P(), P(), P(), P(), P(), P(), P(), P(), P(), P())
    return jax.shard_map(
        local, mesh=mesh, in_specs=in_specs, out_specs=P("row", "col", None), check_vma=False
    )
```
